256 devices in a mesh: group: 4 (over z_hi), resp: 16 (over z_lo, y, core), tensor: 4 (over x).
Axes of the slice: x: 4, y: 4, z: 8 (z_hi: 4, z_lo: 2; z = z_hi * 2 + z_lo), core: 2. Of those that a mesh axis runs over, the one named last changes fastest.
Arguments:
- prompt_rotated_keys: bfloat16 [16384, 1024], P(('group', 'resp'), 'tensor'), parts along dimension 0, may hold values from -420 to 420
- prompt_value_cache: bfloat16 [16384, 1024], P(('group', 'resp'), 'tensor'), parts along dimension 0, may hold values from -6 to 6
- queries: bfloat16 [16384, 8192], P(('group', 'resp', 'tensor')), parts along dimension 0, may hold values from -6 to 6
- response_keys: bfloat16 [16384, 1024], P(('group', 'resp', 'tensor')), parts along dimension 0, may hold values from -6 to 6
- response_values: bfloat16 [16384, 1024], P(('group', 'resp', 'tensor')), parts along dimension 0, may hold values from -6 to 6
- q_gain: float32 [128], replicated, may hold values from 1 to 2
- key_norm_gain: float32 [128], replicated, may hold values from 1 to 2
- prompt_len: int32 [4], P('group'), parts along dimension 0, may hold values from 1024 to 4096
- resp_len: int32 [64], P(('group', 'resp')), parts along dimension 0, may hold values from 64 to 256, as said below
Outputs:
- attended: bfloat16 [16384, 8192], P(('group', 'resp', 'tensor')), parts along dimension 0
The draws below stay inside these ranges and needn't reach their ends.
There are 4 independent parts, one for each index of `group`. The reference program is written for one: setup_inputs(seed, part) draws one part's arguments, and reference() takes and returns one part's arrays. A program takes and returns all parts, laid end to end along the dimension named above; an argument that names none is the same for every part. Nothing has to cross between parts.
Inputs may be any that keep to these rules, and one draw needn't show every extreme that they name: `resp_len`: exactly one response has 256 live positions, the others fewer.
All inputs are finite; a program needn't handle non-finite values.
Results may differ from the reference program's by a relative error of at most 0.014.
Values may be sent and summed in bfloat16 or wider, within the bound.
No kernel may reach another device: no remote copies, remote signals or barrier semaphores. Data moves between devices by JAX's collectives and lax.ppermute only.
A program may use at most 128 MiB of HBM per device.

```python
import jax
import jax.numpy as jnp
from jax import lax

QUERY_HEADS = 64
KEY_VALUE_HEADS = 8
HEAD_SIZE = 128
RESPONSE_LENGTH = 256
RESPONSE_COUNT = 16
PROMPT_LENGTH = 4096


def draw_prompt_rotated_keys(key, part):
    key = jax.random.fold_in(key, 11)
    first_key = jax.random.fold_in(key, 0)
    block_width = KEY_VALUE_HEADS * HEAD_SIZE
    result = jax.random.normal(first_key, (PROMPT_LENGTH, block_width), jnp.float32) * 1.6
    return result.astype(jnp.bfloat16)


def draw_resp_len(key, part):
    key = jax.random.fold_in(key, 23)
    first_key, second_key = jax.random.split(key, 2)
    others = jax.random.randint(first_key, (RESPONSE_COUNT,), RESPONSE_LENGTH // 4, RESPONSE_LENGTH)
    longest = jax.random.randint(second_key, (), 0, RESPONSE_COUNT)
    positions = jnp.arange(RESPONSE_COUNT, dtype=jnp.int32)
    return jnp.where(positions == longest, RESPONSE_LENGTH, others).astype(jnp.int32)


def level_of(stream_key, extent, shards, smallest, high):
    level, own = 1.0, jax.random.fold_in(stream_key, 6)
    for axis_at, shards_of in shards:
        steps = jnp.exp(jax.random.uniform(jax.random.fold_in(own, axis_at), (shards_of,), jnp.float32, smallest / len(shards), high / len(shards)))
        level = level * jnp.repeat(steps, extent[axis_at] // shards_of).reshape([-1 if axis == axis_at else 1 for axis in range(len(extent))])
    return level


def gaussian(key, extent, spread, limit, pieces=(), kind=jnp.bfloat16):
    values = spread * jax.random.normal(key, extent, jnp.float32)
    if pieces:
        values = values * level_of(key, extent, pieces, -0.22, 0.18)
    return jnp.clip(values, -limit, limit).astype(kind)


def setup_inputs(seed: int = 0, part: int = 0) -> dict:
    key_of = jax.random.split(jax.random.key(seed), 10)
    part_splits = jax.random.split(jax.random.fold_in(key_of[9], part), 10)
    prompt_rotated_keys = draw_prompt_rotated_keys(jax.random.fold_in(jax.random.fold_in(key_of[9], part), 71), part)
    prompt_value_cache = gaussian(part_splits[1], (PROMPT_LENGTH, KEY_VALUE_HEADS * HEAD_SIZE), 1.0, 6.0, ((0, 16), (1, 4)))
    queries = gaussian(part_splits[2], (RESPONSE_COUNT * RESPONSE_LENGTH, QUERY_HEADS * HEAD_SIZE), 1.0, 6.0, ((0, 64),))
    response_keys = gaussian(part_splits[3], (RESPONSE_COUNT * RESPONSE_LENGTH, KEY_VALUE_HEADS * HEAD_SIZE), 1.0, 6.0, ((0, 64),))
    response_values = gaussian(part_splits[4], (RESPONSE_COUNT * RESPONSE_LENGTH, KEY_VALUE_HEADS * HEAD_SIZE), 1.0, 6.0, ((0, 64),))
    q_gain = jnp.clip(jax.random.uniform(key_of[5], (HEAD_SIZE,), jnp.float32, 1.0, 2.0), 1.0, 2.0)
    key_norm_gain = jnp.clip(jax.random.uniform(key_of[6], (HEAD_SIZE,), jnp.float32, 1.0, 2.0), 1.0, 2.0)
    prompt_len = jax.random.randint(part_splits[7], (1,), PROMPT_LENGTH // 4, PROMPT_LENGTH + 1).astype(jnp.int32)
    resp_len = draw_resp_len(jax.random.fold_in(jax.random.fold_in(key_of[9], part), 71), part)
    return dict(prompt_rotated_keys=prompt_rotated_keys, prompt_value_cache=prompt_value_cache, queries=queries, response_keys=response_keys, response_values=response_values, q_gain=q_gain, key_norm_gain=key_norm_gain, prompt_len=prompt_len, resp_len=resp_len)


theta_base = 1000000.0
neg_large = -1e+30

def normed_rows(rows, gain, token_positions, heads):
    block_width = rows.shape[1] // heads
    value_matrix = rows.astype(jnp.float32).reshape(rows.shape[0], heads, block_width)
    power = lax.optimization_barrier(jnp.mean(value_matrix * value_matrix, axis=-1, keepdims=True))
    scaled = value_matrix * lax.rsqrt(power + 1e-06) * gain
    half = block_width // 2
    freqs = jnp.power(jnp.float32(theta_base), -jnp.arange(half).astype(jnp.float32) * (2.0 / block_width))
    angles = token_positions.astype(jnp.float32)[:, None] * freqs[None, :]
    cosine = jnp.cos(angles)[:, None, :]
    sine = jnp.sin(angles)[:, None, :]
    first = scaled[..., :half]
    second = scaled[..., half:]
    return jnp.concatenate([first * cosine - second * sine, second * cosine + first * sine], axis=-1)

def reference(prompt_rotated_keys, prompt_value_cache, queries, response_keys, response_values, q_gain, key_norm_gain, prompt_len, resp_len):
    causal_limit = prompt_len[0]
    query_group = QUERY_HEADS // KEY_VALUE_HEADS
    scale = HEAD_SIZE ** (-0.5)
    token_positions = jnp.arange(RESPONSE_LENGTH, dtype=jnp.int32)
    prompt_key_rows = prompt_rotated_keys.astype(jnp.float32).reshape(PROMPT_LENGTH, KEY_VALUE_HEADS, HEAD_SIZE)
    prompt_value_rows = prompt_value_cache.astype(jnp.float32).reshape(PROMPT_LENGTH, KEY_VALUE_HEADS, HEAD_SIZE)
    key_index = jnp.arange(PROMPT_LENGTH + RESPONSE_LENGTH, dtype=jnp.int32)
    own_index = key_index - PROMPT_LENGTH

    def one_response(index):
        length = resp_len[index]
        start = (index * RESPONSE_LENGTH).astype(jnp.int32)
        q_rows = lax.dynamic_slice_in_dim(queries, start, RESPONSE_LENGTH, 0)
        key_rows_local = lax.dynamic_slice_in_dim(response_keys, start, RESPONSE_LENGTH, 0)
        value_rows_local = lax.dynamic_slice_in_dim(response_values, start, RESPONSE_LENGTH, 0)
        query_rows_block = (normed_rows(q_rows, q_gain, causal_limit + token_positions, QUERY_HEADS) * scale).astype(jnp.bfloat16)
        query_rows_block = lax.optimization_barrier(query_rows_block).astype(jnp.float32).reshape(RESPONSE_LENGTH, KEY_VALUE_HEADS, query_group, HEAD_SIZE)
        own_block = normed_rows(key_rows_local, key_norm_gain, causal_limit + token_positions, KEY_VALUE_HEADS).astype(jnp.bfloat16)
        own_block = lax.optimization_barrier(own_block).astype(jnp.float32)
        keys = jnp.concatenate([prompt_key_rows, own_block], axis=0)
        value_matrix = jnp.concatenate([prompt_value_rows, value_rows_local.astype(jnp.float32).reshape(RESPONSE_LENGTH, KEY_VALUE_HEADS, HEAD_SIZE)], axis=0)
        live_prompt = (key_index < causal_limit)[None, :]
        live_self = (key_index[None, :] >= PROMPT_LENGTH) & (own_index[None, :] <= token_positions[:, None]) & (own_index[None, :] < length)
        mask = (live_prompt | live_self)[:, None, None, :]
        scores = jnp.einsum('mgjd,ngd->mgjn', query_rows_block, keys)
        masked = jnp.where(mask, scores, neg_large)
        top = lax.optimization_barrier(jnp.max(masked, axis=-1, keepdims=True))
        weights = jnp.where(mask, jnp.exp(masked - top), 0.0)
        total = lax.optimization_barrier(jnp.sum(weights, axis=-1))
        rounded = lax.optimization_barrier(weights.astype(jnp.bfloat16)).astype(jnp.float32)
        result = jnp.einsum('mgjn,ngd->mgjd', rounded, value_matrix) / total[..., None]
        result = jnp.where((token_positions < length)[:, None, None, None], result, 0.0)
        return result.reshape(RESPONSE_LENGTH, QUERY_HEADS * HEAD_SIZE).astype(jnp.bfloat16)
    outputs = lax.map(one_response, jnp.arange(RESPONSE_COUNT, dtype=jnp.int32))
    return outputs.reshape(RESPONSE_COUNT * RESPONSE_LENGTH, QUERY_HEADS * HEAD_SIZE)
```

```python
import functools

import jax
import jax.numpy as jnp
from jax import lax
from jax.experimental import pallas as pl
from jax.experimental.pallas import tpu as pltpu
from jax.sharding import PartitionSpec as P

HEAD = 128
LENGTH = 256
ROWS = 1024
CHUNK = 1024
LOG2E = 1.4426950408889634
NEG = -1e30
MIB = 1024 * 1024


def nt(a, b):
    return lax.dot_general(a, b, (((1,), (1,)), ((), ())), preferred_element_type=jnp.float32)


def mm(a, b):
    return jnp.dot(a, b, preferred_element_type=jnp.float32)


def prep_kernel(meta, own, r1, r2, r3, aq, bq, ak, bk, q0, q1, rkv):
    t = meta[0]
    wide = jnp.ones((256, 128), jnp.bfloat16)
    at = lax.broadcasted_iota(jnp.int32, (128, 128), 0)
    to = lax.broadcasted_iota(jnp.int32, (128, 128), 1)
    swap = jnp.where((at - to == 64) | (to - at == 64), 1.0, 0.0).astype(jnp.bfloat16)

    def rotated(x, a, b):
        f = x.astype(jnp.float32)
        sq = f * f
        hi = sq.astype(jnp.bfloat16)
        lo = (sq - hi.astype(jnp.float32)).astype(jnp.bfloat16)
        total = mm(jnp.concatenate([hi, lo], axis=1), wide)
        r = lax.rsqrt(total * (1.0 / HEAD) + 1e-06)
        return ((f * a + mm(x, swap) * b) * r).astype(jnp.bfloat16)

    for d, piece in enumerate((own, r1, r2, r3)):
        s = lax.rem(t - d + 4, 4)
        p0 = pl.multiple_of(s * 64, 64)
        rows = pl.ds(p0, 64)
        base = (s // 2) * ROWS + lax.rem(s, 2) * 64
        a8 = jnp.concatenate([aq[rows, :]] * 8, axis=0)
        b8 = jnp.concatenate([bq[rows, :]] * 8, axis=0)
        for h, dst in enumerate((q0, q1)):
            x = jnp.concatenate(
                [piece[:, (h * 8 + j) * 128 : (h * 8 + j + 1) * 128] for j in range(8)], axis=0
            )
            y = rotated(x, a8, b8)
            for j in range(8):
                dst[pl.ds(pl.multiple_of(base + j * 128, 64), 64), :] = y[j * 64 : (j + 1) * 64]
            k = piece[:, 2048 + h * 128 : 2048 + (h + 1) * 128]
            rkv[rows, h * 256 : h * 256 + 128] = rotated(k, ak[rows, :], bk[rows, :])
            rkv[rows, h * 256 + 128 : h * 256 + 256] = piece[
                :, 2304 + h * 128 : 2304 + (h + 1) * 128
            ]


def prep(meta, pieces, tables):
    vmem = pl.BlockSpec(memory_space=pltpu.VMEM)
    return pl.pallas_call(
        prep_kernel,
        out_shape=(
            jax.ShapeDtypeStruct((2048, 128), jnp.bfloat16),
            jax.ShapeDtypeStruct((2048, 128), jnp.bfloat16),
            jax.ShapeDtypeStruct((256, 512), jnp.bfloat16),
        ),
        in_specs=[pl.BlockSpec(memory_space=pltpu.SMEM)] + [vmem] * 8,
        out_specs=(vmem,) * 3,
        compiler_params=pltpu.CompilerParams(vmem_limit_bytes=16 * MIB),
        cost_estimate=pl.CostEstimate(flops=10**9, bytes_accessed=3 * 10**6, transcendentals=10**6),
        name="prep",
    )(meta, *pieces, *tables)


def lanes(x, f, start):
    for i in range(x.shape[1] // 128):
        start = f(start, x[:, i * 128 : (i + 1) * 128])
    return start


def attend_kernel(heads, first, last, layout, *refs):
    it = iter(refs)
    meta = next(it)
    qs = [next(it) for _ in heads]
    rkv = next(it) if first else None
    pieces = [next(it) for _ in layout]
    states = [[next(it) for _ in range(3)] for _ in heads] if not first else None
    outs = [[next(it) for _ in range(4)] if last else [next(it) for _ in range(3)] for _ in heads]
    kvs, bias, m_s, mx_s, l_s, acc_s, sa, sb, oa, ob, sems = it
    plen, rlen, t, core = meta[0], meta[1], meta[2], meta[3]
    chips = 1 + max(i for i, _, _, _ in layout)
    slots, live = [], 0
    for i in range(chips):
        is_live = (meta[4 + i] < plen).astype(jnp.int32)
        dead = i - live
        slots.append(jnp.where(is_live == 1, live, chips - 1 - dead))
        live = live + is_live
    steps = (live * 512 + CHUNK - 1) // CHUNK
    copies = []
    for n, (piece, (i, other, row, count)) in enumerate(zip(pieces, layout)):
        c = 1 - core if other else core
        to = pl.multiple_of(slots[i] * 512 + c * 256 + row, 128)
        for k, h in enumerate(heads):
            copy = pltpu.make_async_copy(
                piece.at[:, pl.ds(h * 256, 256)],
                kvs.at[k, pl.ds(to, count), :],
                sems.at[n * len(heads) + k],
            )
            copy.start()
            copies.append(copy)
    for i in range(chips):
        at = lax.broadcasted_iota(jnp.int32, (8, 512), 1) + meta[4 + i]
        bias[slots[i]] = jnp.where(at < plen, 0.0, NEG)

    s_bufs, o_bufs = (sa, sb), (oa, ob)
    tiles = [(k, p) for k in range(len(heads)) for p in range(2)]

    def rows_of(p):
        return slice(p * ROWS, (p + 1) * ROWS)

    def begin1(n):
        k, p = tiles[n]
        if first:
            h = heads[k]
            s = nt(qs[k][rows_of(p), :], rkv[:, h * 256 : h * 256 + 128])
            key = lax.broadcasted_iota(jnp.int32, (ROWS, 256), 1)
            pos = p * 128 + lax.rem(lax.broadcasted_iota(jnp.int32, (ROWS, 256), 0), 128)
            s = jnp.where((key <= pos) & (key < rlen), s, NEG)
            o_bufs[n % 2][...] = s
            m_s[...] = jnp.maximum(s[:, :128], s[:, 128:])
        else:
            m_s[...] = states[k][0][rows_of(p), :]

    def pass1(n, c):
        k, p = tiles[n]
        keys = kvs[k, pl.ds(pl.multiple_of(c * CHUNK, CHUNK), CHUNK), 0:128]
        add = jnp.concatenate([bias[2 * c], bias[2 * c + 1]], axis=1)[0:1, :]
        s = nt(qs[k][rows_of(p), :], keys) + add
        s_bufs[n % 2][c] = s
        m_s[...] = lanes(s, jnp.maximum, m_s[...])

    def weigh(s, m):
        return jnp.concatenate(
            [
                jnp.exp2((s[:, i * 128 : (i + 1) * 128] - m) * LOG2E)
                for i in range(s.shape[1] // 128)
            ],
            axis=1,
        )

    def begin2(n):
        k, p = tiles[n]
        m = jnp.broadcast_to(jnp.max(m_s[...], axis=-1, keepdims=True), (ROWS, 128))
        mx_s[...] = m
        if first:
            h = heads[k]
            w = weigh(o_bufs[n % 2][...], m)
            l_s[...] = w[:, :128] + w[:, 128:]
            acc_s[...] = mm(w.astype(jnp.bfloat16), rkv[:, h * 256 + 128 : h * 256 + 256])
        else:
            old = jnp.exp2((states[k][0][rows_of(p), :] - m) * LOG2E)
            l_s[...] = states[k][1][rows_of(p), :] * old
            acc_s[...] = states[k][2][rows_of(p), :] * old

    def pass2(n, c):
        k, _ = tiles[n]
        values = kvs[k, pl.ds(pl.multiple_of(c * CHUNK, CHUNK), CHUNK), 128:256]
        w = weigh(s_bufs[n % 2][c], mx_s[...])
        l_s[...] = lanes(w, jnp.add, l_s[...])
        acc_s[...] += mm(w.astype(jnp.bfloat16), values)

    def finish(n):
        k, p = tiles[n]
        if not last:
            for ref, x in zip(outs[k], (mx_s, l_s, acc_s)):
                ref[rows_of(p), :] = x[...]
            return
        total = jnp.sum(l_s[...], axis=-1, keepdims=True)
        res = acc_s[...] / total
        pos = p * 128 + lax.rem(lax.broadcasted_iota(jnp.int32, (ROWS, 128), 0), 128)
        res = jnp.where(pos < rlen, res, 0.0).astype(jnp.bfloat16)
        for half in range(2):
            d = lax.rem(p * 2 + half - t + 4, 4)
            for e in range(4):

                @pl.when(d == e)
                def _():
                    for j in range(8):
                        r = j * 128 + half * 64
                        outs[k][e][:, j * 128 : (j + 1) * 128] = res[r : r + 64]

    begin1(0)
    for copy in copies:
        copy.wait()

    def loop(f):
        lax.fori_loop(0, steps, lambda c, z: (f(c), z)[1], 0)

    loop(lambda c: pass1(0, c))
    for n in range(len(tiles)):
        begin2(n)
        if n + 1 < len(tiles):
            begin1(n + 1)

            def both(c):
                pass1(n + 1, c)
                pass2(n, c)

            loop(both)
        else:
            loop(lambda c: pass2(n, c))
        finish(n)


def attend(heads, first, last, layout, meta, qs, rkv, pieces, states):
    vmem = pl.BlockSpec(memory_space=pltpu.VMEM)
    anywhere = pl.BlockSpec(memory_space=pl.ANY)
    chips = 1 + max(i for i, _, _, _ in layout)
    state = jax.ShapeDtypeStruct((2048, 128), jnp.float32)
    if last:
        out_shape = [jax.ShapeDtypeStruct((64, 1024), jnp.bfloat16)] * (4 * len(heads))
    else:
        out_shape = [state] * (3 * len(heads))
    steps = chips * 512 // CHUNK
    f32 = jnp.float32
    scratch = [
        pltpu.VMEM((len(heads), chips * 512, 256), jnp.bfloat16),
        pltpu.VMEM((chips, 8, 512), f32),
        *[pltpu.VMEM((ROWS, 128), f32)] * 4,
        *[pltpu.VMEM((steps, ROWS, CHUNK), f32)] * 2,
        *[pltpu.VMEM((ROWS if first else 8, 256), f32)] * 2,
        pltpu.SemaphoreType.DMA((len(layout) * len(heads),)),
    ]
    args = [meta, *qs] + ([rkv] if first else []) + list(pieces)
    specs = [pl.BlockSpec(memory_space=pltpu.SMEM)] + [vmem] * len(qs)
    specs += ([vmem] if first else []) + [anywhere] * len(pieces)
    if not first:
        args += [x for s in states for x in s]
        specs += [vmem] * (3 * len(heads))
    keys = chips * 512 + (256 if first else 0)
    return pl.pallas_call(
        functools.partial(attend_kernel, heads, first, last, layout),
        out_shape=tuple(out_shape),
        in_specs=specs,
        out_specs=(vmem,) * len(out_shape),
        scratch_shapes=scratch,
        compiler_params=pltpu.CompilerParams(vmem_limit_bytes=44 * MIB),
        cost_estimate=pl.CostEstimate(
            flops=8 * 2048 * keys * 128 * len(heads),
            bytes_accessed=4 * MIB,
            transcendentals=2048 * keys * len(heads),
        ),
        name="attend",
    )(*args)


def gather_kernel(meta, *refs):
    pieces, out, sems = refs[:8], refs[8], refs[9]
    t = meta[0]
    copies = []
    for n, piece in enumerate(pieces):
        h, d = n // 4, n % 4
        to = pl.multiple_of(lax.rem(t - d + 4, 4) * 2048 + h * 1024, 1024)
        copy = pltpu.make_async_copy(piece, out.at[:, pl.ds(to, 1024)], sems.at[n])
        copy.start()
        copies.append(copy)
    for copy in copies:
        copy.wait()


def assemble(meta, pieces):
    return pl.pallas_call(
        gather_kernel,
        out_shape=jax.ShapeDtypeStruct((64, 8192), jnp.bfloat16),
        in_specs=[pl.BlockSpec(memory_space=pltpu.SMEM)] + [pl.BlockSpec(memory_space=pl.ANY)] * 8,
        out_specs=pl.BlockSpec(memory_space=pl.ANY),
        scratch_shapes=[pltpu.SemaphoreType.DMA((8,))],
        name="assemble",
    )(meta, *pieces)


def place(z, y, c):
    return z * 8 + y * 2 + c


def move(x, dz, dy, dc=0):
    pairs = [
        (place(z, y, c), place(z ^ dz, (y + dy) % 4, c ^ dc))
        for z in range(2)
        for y in range(4)
        for c in range(2)
    ]
    return lax.ppermute(x, "resp", pairs)


def shift(x, d):
    return lax.ppermute(x, "tensor", [(i, (i + d) % 4) for i in range(4)])


def per_device(pk, pv, queries, rk, rv, q_gain, k_gain, prompt_len, resp_len):
    plen, rlen = prompt_len[0], resp_len[0]
    t = lax.axis_index("tensor")
    r = lax.axis_index("resp")
    core, y, z = r % 2, (r // 2) % 4, r // 8

    kv = jnp.concatenate([pk[:, :128], pv[:, :128], pk[:, 128:], pv[:, 128:]], axis=1)
    kz, ka, kb = move(kv, 1, 0), move(kv, 0, 1), move(kv, 0, 3)

    def for_dst(d):
        u = lax.rem(t + d, 4)
        return jnp.concatenate(
            [
                lax.dynamic_slice_in_dim(queries, u * 2048, 2048, 1),
                lax.dynamic_slice_in_dim(rk, u * 256, 256, 1),
                lax.dynamic_slice_in_dim(rv, u * 256, 256, 1),
            ],
            axis=1,
        )

    q_pieces = [for_dst(0)] + [shift(for_dst(d), d) for d in (1, 2, 3)]

    kza, kzb = move(kz, 0, 1), move(kz, 0, 3)
    kaa, kbb = move(ka[:128], 0, 1), move(kb[128:], 0, 3)
    kzaa, kzbb = move(kza[:128], 0, 1), move(kzb[128:], 0, 3)

    half = HEAD // 2
    pos = (plen + jnp.arange(LENGTH, dtype=jnp.int32)).astype(jnp.float32)
    freqs = jnp.power(
        jnp.float32(1000000.0), -jnp.arange(half).astype(jnp.float32) * (2.0 / HEAD)
    )
    angles = pos[:, None] * freqs[None, :]
    cosine, sine = jnp.cos(angles), jnp.sin(angles)
    c2 = jnp.concatenate([cosine, cosine], axis=1)
    s2 = jnp.concatenate([-sine, sine], axis=1)
    scale = HEAD ** (-0.5)
    tables = (
        c2 * (q_gain * scale),
        s2 * (jnp.roll(q_gain, half) * scale),
        c2 * k_gain,
        s2 * jnp.roll(k_gain, half),
    )
    q0, q1, rkv = prep(jnp.stack([t]), q_pieces, tables)

    def base(dz, dy):
        return ((z + dz) % 2 * 4 + (y + dy) % 4) * 512

    def meta(chips):
        return jnp.stack([plen, rlen, t, core] + [base(dz, dy) for dz, dy in chips]).astype(
            jnp.int32
        )

    def both(pieces):
        return list(pieces) + [move(x, 0, 0, 1) for x in pieces]

    one = both([kv, kz, ka, kb])
    layout_one = [(i, o, 0, 256) for o in range(2) for i in range(4)]
    two = both([kza, kzb, kaa, kbb, kzaa, kzbb])
    layout_two = [
        (i, o, row, count)
        for o in range(2)
        for i, row, count in (
            (0, 0, 256),
            (1, 0, 256),
            (2, 0, 128),
            (2, 128, 128),
            (3, 0, 128),
            (3, 128, 128),
        )
    ]
    meta_one = meta([(0, 0), (1, 0), (0, -1), (0, 1)])
    meta_two = meta([(1, -1), (1, 1), (0, 2), (1, 2)])
    st = attend((0, 1), True, False, layout_one, meta_one, (q0, q1), rkv, one, None)
    pieces = []
    for h, q in enumerate((q0, q1)):
        o = attend(
            (h,), False, True, layout_two, meta_two, (q,), None, two, [st[3 * h : 3 * h + 3]]
        )
        pieces += [o[0]] + [shift(o[d], d) for d in (1, 2, 3)]
    return assemble(jnp.stack([t]), pieces)


def solution(mesh):
    rows = P(("group", "resp", "tensor"), None)
    cache = P(("group", "resp"), "tensor")
    in_specs = (cache, cache, rows, rows, rows, P(), P(), P("group"), P(("group", "resp")))
    return jax.shard_map(
        per_device, mesh=mesh, in_specs=in_specs, out_specs=rows, check_vma=False
    )
```

```python
import functools

import jax
import jax.numpy as jnp
from jax import lax
from jax.experimental import pallas as pl
from jax.experimental.pallas import tpu as pltpu
from jax.sharding import PartitionSpec as P

HEAD = 128
LENGTH = 256
ROWS = 1024
CHUNK = 1024
LOG2E = 1.4426950408889634
NEG = -1e30
MIB = 1024 * 1024


def nt(a, b):
    return lax.dot_general(a, b, (((1,), (1,)), ((), ())), preferred_element_type=jnp.float32)


def mm(a, b):
    return jnp.dot(a, b, preferred_element_type=jnp.float32)


def split_kernel(meta, pk, pv, queries, rk, rv, own, q1, q2, q3, kv):
    t = meta[0]
    for d, dst in enumerate((own, q1, q2, q3)):
        u = lax.rem(t + d, 4)
        dst[:, :2048] = queries[:, pl.ds(pl.multiple_of(u * 2048, 2048), 2048)]
        dst[:, 2048:2304] = rk[:, pl.ds(pl.multiple_of(u * 256, 256), 256)]
        dst[:, 2304:] = rv[:, pl.ds(pl.multiple_of(u * 256, 256), 256)]
    for h in range(2):
        kv[:, h * 256 : h * 256 + 128] = pk[:, h * 128 : (h + 1) * 128]
        kv[:, h * 256 + 128 : h * 256 + 256] = pv[:, h * 128 : (h + 1) * 128]


def split(meta, *args):
    vmem = pl.BlockSpec(memory_space=pltpu.VMEM)
    piece = jax.ShapeDtypeStruct((64, 2560), jnp.bfloat16)
    return pl.pallas_call(
        split_kernel,
        out_shape=(piece,) * 4 + (jax.ShapeDtypeStruct((256, 512), jnp.bfloat16),),
        in_specs=[pl.BlockSpec(memory_space=pltpu.SMEM)] + [vmem] * 5,
        out_specs=(vmem,) * 5,
        compiler_params=pltpu.CompilerParams(vmem_limit_bytes=16 * MIB),
        name="split",
    )(meta, *args)


def prep_kernel(meta, own, r1, r2, r3, aq, bq, ak, bk, q0, q1, rkv):
    t = meta[0]
    wide = jnp.ones((256, 128), jnp.bfloat16)
    at = lax.broadcasted_iota(jnp.int32, (128, 128), 0)
    to = lax.broadcasted_iota(jnp.int32, (128, 128), 1)
    swap = jnp.where((at - to == 64) | (to - at == 64), 1.0, 0.0).astype(jnp.bfloat16)

    def rotated(x, a, b):
        f = x.astype(jnp.float32)
        sq = f * f
        hi = sq.astype(jnp.bfloat16)
        lo = (sq - hi.astype(jnp.float32)).astype(jnp.bfloat16)
        total = mm(jnp.concatenate([hi, lo], axis=1), wide)
        r = lax.rsqrt(total * (1.0 / HEAD) + 1e-06)
        return ((f * a + mm(x, swap) * b) * r).astype(jnp.bfloat16)

    for d, piece in enumerate((own, r1, r2, r3)):
        s = lax.rem(t - d + 4, 4)
        p0 = pl.multiple_of(s * 64, 64)
        rows = pl.ds(p0, 64)
        base = (s // 2) * ROWS + lax.rem(s, 2) * 64
        a8 = jnp.concatenate([aq[rows, :]] * 8, axis=0)
        b8 = jnp.concatenate([bq[rows, :]] * 8, axis=0)
        for h, dst in enumerate((q0, q1)):
            x = jnp.concatenate(
                [piece[:, (h * 8 + j) * 128 : (h * 8 + j + 1) * 128] for j in range(8)], axis=0
            )
            y = rotated(x, a8, b8)
            for j in range(8):
                dst[pl.ds(pl.multiple_of(base + j * 128, 64), 64), :] = y[j * 64 : (j + 1) * 64]
            k = piece[:, 2048 + h * 128 : 2048 + (h + 1) * 128]
            rkv[rows, h * 256 : h * 256 + 128] = rotated(k, ak[rows, :], bk[rows, :])
            rkv[rows, h * 256 + 128 : h * 256 + 256] = piece[
                :, 2304 + h * 128 : 2304 + (h + 1) * 128
            ]


def prep(meta, pieces, tables):
    vmem = pl.BlockSpec(memory_space=pltpu.VMEM)
    return pl.pallas_call(
        prep_kernel,
        out_shape=(
            jax.ShapeDtypeStruct((2048, 128), jnp.bfloat16),
            jax.ShapeDtypeStruct((2048, 128), jnp.bfloat16),
            jax.ShapeDtypeStruct((256, 512), jnp.bfloat16),
        ),
        in_specs=[pl.BlockSpec(memory_space=pltpu.SMEM)] + [vmem] * 8,
        out_specs=(vmem,) * 3,
        compiler_params=pltpu.CompilerParams(vmem_limit_bytes=16 * MIB),
        cost_estimate=pl.CostEstimate(flops=10**9, bytes_accessed=3 * 10**6, transcendentals=10**6),
        name="prep",
    )(meta, *pieces, *tables)


def lanes(x, f, start):
    for i in range(x.shape[1] // 128):
        start = f(start, x[:, i * 128 : (i + 1) * 128])
    return start


def attend_kernel(heads, first, last, layout, *refs):
    it = iter(refs)
    meta = next(it)
    qs = [next(it) for _ in heads]
    rkv = next(it) if first else None
    pieces = [next(it) for _ in layout]
    states = [[next(it) for _ in range(3)] for _ in heads] if not first else None
    outs = [[next(it) for _ in range(4)] if last else [next(it) for _ in range(3)] for _ in heads]
    kvs, bias, m_s, mx_s, l_s, acc_s, sa, sb, oa, ob, sems = it
    plen, rlen, t, core = meta[0], meta[1], meta[2], meta[3]
    chips = 1 + max(i for i, _, _, _ in layout)
    slots, live = [], 0
    for i in range(chips):
        is_live = (meta[4 + i] < plen).astype(jnp.int32)
        dead = i - live
        slots.append(jnp.where(is_live == 1, live, chips - 1 - dead))
        live = live + is_live
    steps = (live * 512 + CHUNK - 1) // CHUNK
    copies = []
    for n, (piece, (i, other, row, count)) in enumerate(zip(pieces, layout)):
        c = 1 - core if other else core
        to = pl.multiple_of(slots[i] * 512 + c * 256 + row, 128)
        for k, h in enumerate(heads):
            copy = pltpu.make_async_copy(
                piece.at[:, pl.ds(h * 256, 256)],
                kvs.at[k, pl.ds(to, count), :],
                sems.at[n * len(heads) + k],
            )
            copy.start()
            copies.append(copy)
    for i in range(chips):
        at = lax.broadcasted_iota(jnp.int32, (8, 512), 1) + meta[4 + i]
        bias[slots[i]] = jnp.where(at < plen, 0.0, NEG)

    s_bufs, o_bufs = (sa, sb), (oa, ob)
    tiles = [(k, p) for k in range(len(heads)) for p in range(2)]

    def rows_of(p):
        return slice(p * ROWS, (p + 1) * ROWS)

    def begin1(n):
        k, p = tiles[n]
        if first:
            h = heads[k]
            s = nt(qs[k][rows_of(p), :], rkv[:, h * 256 : h * 256 + 128])
            key = lax.broadcasted_iota(jnp.int32, (ROWS, 256), 1)
            pos = p * 128 + lax.rem(lax.broadcasted_iota(jnp.int32, (ROWS, 256), 0), 128)
            s = jnp.where((key <= pos) & (key < rlen), s, NEG)
            o_bufs[n % 2][...] = s
            m_s[...] = jnp.maximum(s[:, :128], s[:, 128:])
        else:
            m_s[...] = states[k][0][rows_of(p), :]

    def pass1(n, c):
        k, p = tiles[n]
        keys = kvs[k, pl.ds(pl.multiple_of(c * CHUNK, CHUNK), CHUNK), 0:128]
        add = jnp.concatenate([bias[2 * c], bias[2 * c + 1]], axis=1)[0:1, :]
        s = nt(qs[k][rows_of(p), :], keys) + add
        s_bufs[n % 2][c] = s
        m_s[...] = lanes(s, jnp.maximum, m_s[...])

    def weigh(s, m):
        return jnp.concatenate(
            [
                jnp.exp2((s[:, i * 128 : (i + 1) * 128] - m) * LOG2E)
                for i in range(s.shape[1] // 128)
            ],
            axis=1,
        )

    def begin2(n):
        k, p = tiles[n]
        m = jnp.broadcast_to(jnp.max(m_s[...], axis=-1, keepdims=True), (ROWS, 128))
        mx_s[...] = m
        if first:
            h = heads[k]
            w = weigh(o_bufs[n % 2][...], m)
            l_s[...] = w[:, :128] + w[:, 128:]
            acc_s[...] = mm(w.astype(jnp.bfloat16), rkv[:, h * 256 + 128 : h * 256 + 256])
        else:
            old = jnp.exp2((states[k][0][rows_of(p), :] - m) * LOG2E)
            l_s[...] = states[k][1][rows_of(p), :] * old
            acc_s[...] = states[k][2][rows_of(p), :] * old

    def pass2(n, c):
        k, _ = tiles[n]
        values = kvs[k, pl.ds(pl.multiple_of(c * CHUNK, CHUNK), CHUNK), 128:256]
        w = weigh(s_bufs[n % 2][c], mx_s[...])
        l_s[...] = lanes(w, jnp.add, l_s[...])
        acc_s[...] += mm(w.astype(jnp.bfloat16), values)

    def finish(n):
        k, p = tiles[n]
        if not last:
            for ref, x in zip(outs[k], (mx_s, l_s, acc_s)):
                ref[rows_of(p), :] = x[...]
            return
        total = jnp.sum(l_s[...], axis=-1, keepdims=True)
        res = acc_s[...] / total
        pos = p * 128 + lax.rem(lax.broadcasted_iota(jnp.int32, (ROWS, 128), 0), 128)
        res = jnp.where(pos < rlen, res, 0.0).astype(jnp.bfloat16)
        for half in range(2):
            d = lax.rem(p * 2 + half - t + 4, 4)
            for e in range(4):

                @pl.when(d == e)
                def _():
                    for j in range(8):
                        r = j * 128 + half * 64
                        outs[k][e][:, j * 128 : (j + 1) * 128] = res[r : r + 64]

    begin1(0)
    for copy in copies:
        copy.wait()

    def loop(f):
        lax.fori_loop(0, steps, lambda c, z: (f(c), z)[1], 0)

    loop(lambda c: pass1(0, c))
    for n in range(len(tiles)):
        begin2(n)
        if n + 1 < len(tiles):
            begin1(n + 1)

            def both(c):
                pass1(n + 1, c)
                pass2(n, c)

            loop(both)
        else:
            loop(lambda c: pass2(n, c))
        finish(n)


def attend(heads, first, last, layout, meta, qs, rkv, pieces, states):
    vmem = pl.BlockSpec(memory_space=pltpu.VMEM)
    anywhere = pl.BlockSpec(memory_space=pl.ANY)
    chips = 1 + max(i for i, _, _, _ in layout)
    state = jax.ShapeDtypeStruct((2048, 128), jnp.float32)
    if last:
        out_shape = [jax.ShapeDtypeStruct((64, 1024), jnp.bfloat16)] * (4 * len(heads))
    else:
        out_shape = [state] * (3 * len(heads))
    steps = chips * 512 // CHUNK
    f32 = jnp.float32
    scratch = [
        pltpu.VMEM((len(heads), chips * 512, 256), jnp.bfloat16),
        pltpu.VMEM((chips, 8, 512), f32),
        *[pltpu.VMEM((ROWS, 128), f32)] * 4,
        *[pltpu.VMEM((steps, ROWS, CHUNK), f32)] * 2,
        *[pltpu.VMEM((ROWS if first else 8, 256), f32)] * 2,
        pltpu.SemaphoreType.DMA((len(layout) * len(heads),)),
    ]
    args = [meta, *qs] + ([rkv] if first else []) + list(pieces)
    specs = [pl.BlockSpec(memory_space=pltpu.SMEM)] + [vmem] * len(qs)
    specs += ([vmem] if first else []) + [anywhere] * len(pieces)
    if not first:
        args += [x for s in states for x in s]
        specs += [vmem] * (3 * len(heads))
    keys = chips * 512 + (256 if first else 0)
    return pl.pallas_call(
        functools.partial(attend_kernel, heads, first, last, layout),
        out_shape=tuple(out_shape),
        in_specs=specs,
        out_specs=(vmem,) * len(out_shape),
        scratch_shapes=scratch,
        compiler_params=pltpu.CompilerParams(vmem_limit_bytes=32 * MIB),
        cost_estimate=pl.CostEstimate(
            flops=8 * 2048 * keys * 128 * len(heads),
            bytes_accessed=4 * MIB,
            transcendentals=2048 * keys * len(heads),
        ),
        name="attend",
    )(*args)


def gather_kernel(meta, *refs):
    pieces, out = refs[:8], refs[8]
    t = meta[0]
    for n, piece in enumerate(pieces):
        h, d = n // 4, n % 4
        to = pl.multiple_of(lax.rem(t - d + 4, 4) * 2048 + h * 1024, 1024)
        out[:, pl.ds(to, 1024)] = piece[...]


def assemble(meta, pieces):
    vmem = pl.BlockSpec(memory_space=pltpu.VMEM)
    return pl.pallas_call(
        gather_kernel,
        out_shape=jax.ShapeDtypeStruct((64, 8192), jnp.bfloat16),
        in_specs=[pl.BlockSpec(memory_space=pltpu.SMEM)] + [vmem] * 8,
        out_specs=vmem,
        compiler_params=pltpu.CompilerParams(vmem_limit_bytes=16 * MIB),
        name="assemble",
    )(meta, *pieces)


def place(z, y, c):
    return z * 8 + y * 2 + c


def move(x, dz, dy, dc=0):
    pairs = [
        (place(z, y, c), place(z ^ dz, (y + dy) % 4, c ^ dc))
        for z in range(2)
        for y in range(4)
        for c in range(2)
    ]
    return lax.ppermute(x, "resp", pairs)


def shift(x, d):
    return lax.ppermute(x, "tensor", [(i, (i + d) % 4) for i in range(4)])


def per_device(pk, pv, queries, rk, rv, q_gain, k_gain, prompt_len, resp_len):
    plen, rlen = prompt_len[0], resp_len[0]
    t = lax.axis_index("tensor")
    r = lax.axis_index("resp")
    core, y, z = r % 2, (r // 2) % 4, r // 8

    *mine, kv = split(jnp.stack([t]), pk, pv, queries, rk, rv)
    q_pieces = [mine[0]] + [shift(mine[d], d) for d in (1, 2, 3)]
    kz, ka, kb, ks = move(kv, 1, 0), move(kv, 0, 1), move(kv, 0, 3), move(kv, 0, 2)
    kza, kzb, kzs = move(kz, 0, 1), move(kz, 0, 3), move(kz, 0, 2)

    half = HEAD // 2
    pos = (plen + jnp.arange(LENGTH, dtype=jnp.int32)).astype(jnp.float32)
    freqs = jnp.power(
        jnp.float32(1000000.0), -jnp.arange(half).astype(jnp.float32) * (2.0 / HEAD)
    )
    angles = pos[:, None] * freqs[None, :]
    cosine, sine = jnp.cos(angles), jnp.sin(angles)
    c2 = jnp.concatenate([cosine, cosine], axis=1)
    s2 = jnp.concatenate([-sine, sine], axis=1)
    scale = HEAD ** (-0.5)
    tables = (
        c2 * (q_gain * scale),
        s2 * (jnp.roll(q_gain, half) * scale),
        c2 * k_gain,
        s2 * jnp.roll(k_gain, half),
    )
    q0, q1, rkv = prep(jnp.stack([t]), q_pieces, tables)

    def base(dz, dy):
        return ((z + dz) % 2 * 4 + (y + dy) % 4) * 512

    def meta(chips):
        return jnp.stack([plen, rlen, t, core] + [base(dz, dy) for dz, dy in chips]).astype(
            jnp.int32
        )

    def both(pieces):
        return list(pieces) + [move(x, 0, 0, 1) for x in pieces]

    layout = [(i, o, 0, 256) for o in range(2) for i in range(4)]
    one = both([kv, kz, ka, kb])
    meta_one = meta([(0, 0), (1, 0), (0, -1), (0, 1)])
    meta_two = meta([(1, -1), (1, 1), (0, 2), (1, 2)])
    st0 = attend((0,), True, False, layout, meta_one, (q0,), rkv, one, None)
    (kza, kzb, ks, kzs), st0 = lax.optimization_barrier(((kza, kzb, ks, kzs), st0))
    two = both([kza, kzb, ks, kzs])
    st1 = attend((1,), True, False, layout, meta_one, (q1,), rkv, one, None)
    pieces = []
    for h, q, st in ((0, q0, st0), (1, q1, st1)):
        o = attend((h,), False, True, layout, meta_two, (q,), None, two, [st])
        pieces += [o[0]] + [shift(o[d], d) for d in (1, 2, 3)]
    return assemble(jnp.stack([t]), pieces)


def solution(mesh):
    rows = P(("group", "resp", "tensor"), None)
    cache = P(("group", "resp"), "tensor")
    in_specs = (cache, cache, rows, rows, rows, P(), P(), P("group"), P(("group", "resp")))
    return jax.shard_map(
        per_device, mesh=mesh, in_specs=in_specs, out_specs=rows, check_vma=False
    )
```

```python
import functools

import jax
import jax.numpy as jnp
from jax import lax
from jax.experimental import pallas as pl
from jax.experimental.pallas import tpu as pltpu
from jax.sharding import PartitionSpec as P

HEAD = 128
LENGTH = 256
ROWS = 1024
CHUNK = 1024
LOG2E = 1.4426950408889634
NEG = -1e30
MIB = 1024 * 1024


def nt(a, b):
    return lax.dot_general(a, b, (((1,), (1,)), ((), ())), preferred_element_type=jnp.float32)


def mm(a, b):
    return jnp.dot(a, b, preferred_element_type=jnp.float32)


def split_kernel(meta, pk, pv, queries, rk, rv, own, q1, q2, q3, kv, sems):
    t = meta[2]
    copies = []

    def copy(src, dst):
        copies.append(pltpu.make_async_copy(src, dst, sems.at[len(copies)]))
        copies[-1].start()

    for d, dst in ((2, q2), (1, q1), (3, q3), (0, own)):
        u = lax.rem(t + d, 4)
        copy(
            queries.at[:, pl.ds(pl.multiple_of(u * 2048, 2048), 2048)], dst.at[:, pl.ds(0, 2048)]
        )
        copy(rk.at[:, pl.ds(pl.multiple_of(u * 256, 256), 256)], dst.at[:, pl.ds(2048, 256)])
        copy(rv.at[:, pl.ds(pl.multiple_of(u * 256, 256), 256)], dst.at[:, pl.ds(2304, 256)])
    for h in range(2):
        copy(pk.at[:, pl.ds(h * 128, 128)], kv.at[:, pl.ds(h * 256, 128)])
        copy(pv.at[:, pl.ds(h * 128, 128)], kv.at[:, pl.ds(h * 256 + 128, 128)])
    for c in copies:
        c.wait()


def split(meta, *args):
    vmem = pl.BlockSpec(memory_space=pltpu.VMEM)
    piece = jax.ShapeDtypeStruct((64, 2560), jnp.bfloat16)
    return pl.pallas_call(
        split_kernel,
        out_shape=(piece,) * 4 + (jax.ShapeDtypeStruct((256, 512), jnp.bfloat16),),
        in_specs=[pl.BlockSpec(memory_space=pltpu.SMEM)] + [pl.BlockSpec(memory_space=pl.ANY)] * 5,
        out_specs=(vmem,) * 5,
        scratch_shapes=[pltpu.SemaphoreType.DMA((16,))],
        compiler_params=pltpu.CompilerParams(vmem_limit_bytes=56 * MIB),
        name="split",
    )(meta, *args)


def prep_kernel(meta, own, r1, r2, r3, aq, bq, ak, bk, q0, q1, rkv):
    t = meta[2]
    wide = jnp.ones((256, 128), jnp.bfloat16)
    at = lax.broadcasted_iota(jnp.int32, (128, 128), 0)
    to = lax.broadcasted_iota(jnp.int32, (128, 128), 1)
    swap = jnp.where((at - to == 64) | (to - at == 64), 1.0, 0.0).astype(jnp.bfloat16)

    def rotated(x, a, b):
        f = x.astype(jnp.float32)
        sq = f * f
        hi = sq.astype(jnp.bfloat16)
        lo = (sq - hi.astype(jnp.float32)).astype(jnp.bfloat16)
        total = mm(jnp.concatenate([hi, lo], axis=1), wide)
        r = lax.rsqrt(total * (1.0 / HEAD) + 1e-06)
        return ((f * a + mm(x, swap) * b) * r).astype(jnp.bfloat16)

    for d, piece in enumerate((own, r1, r2, r3)):
        s = lax.rem(t - d + 4, 4)
        p0 = pl.multiple_of(s * 64, 64)
        rows = pl.ds(p0, 64)
        base = (s // 2) * ROWS + lax.rem(s, 2) * 64
        a8 = jnp.concatenate([aq[rows, :]] * 8, axis=0)
        b8 = jnp.concatenate([bq[rows, :]] * 8, axis=0)
        for h, dst in enumerate((q0, q1)):
            x = jnp.concatenate(
                [piece[:, (h * 8 + j) * 128 : (h * 8 + j + 1) * 128] for j in range(8)], axis=0
            )
            y = rotated(x, a8, b8)
            for j in range(8):
                dst[pl.ds(pl.multiple_of(base + j * 128, 64), 64), :] = y[j * 64 : (j + 1) * 64]
            k = piece[:, 2048 + h * 128 : 2048 + (h + 1) * 128]
            rkv[rows, h * 256 : h * 256 + 128] = rotated(k, ak[rows, :], bk[rows, :])
            rkv[rows, h * 256 + 128 : h * 256 + 256] = piece[
                :, 2304 + h * 128 : 2304 + (h + 1) * 128
            ]


def prep(meta, pieces, tables):
    vmem = pl.BlockSpec(memory_space=pltpu.VMEM)
    return pl.pallas_call(
        prep_kernel,
        out_shape=(
            jax.ShapeDtypeStruct((2048, 128), jnp.bfloat16),
            jax.ShapeDtypeStruct((2048, 128), jnp.bfloat16),
            jax.ShapeDtypeStruct((256, 512), jnp.bfloat16),
        ),
        in_specs=[pl.BlockSpec(memory_space=pltpu.SMEM)] + [vmem] * 8,
        out_specs=(vmem,) * 3,
        compiler_params=pltpu.CompilerParams(vmem_limit_bytes=16 * MIB),
        cost_estimate=pl.CostEstimate(flops=10**9, bytes_accessed=3 * 10**6, transcendentals=10**6),
        name="prep",
    )(meta, *pieces, *tables)


def lanes(x, f, start):
    for i in range(x.shape[1] // 128):
        start = f(start, x[:, i * 128 : (i + 1) * 128])
    return start


def attend_kernel(heads, first, last, layout, where, *refs):
    it = iter(refs)
    meta = next(it)
    qs = [next(it) for _ in heads]
    rkv = next(it) if first else None
    pieces = [next(it) for _ in layout]
    states = [[next(it) for _ in range(3)] for _ in heads] if not first else None
    outs = [[next(it) for _ in range(4)] if last else [next(it) for _ in range(3)] for _ in heads]
    kvs, bias, m_s, mx_s, l_s, acc_s, sa, sb, oa, ob, sems = it
    plen, rlen, t, r = meta[0], meta[1], meta[2], meta[3]
    core, y, z = r & 1, (r >> 1) & 3, r >> 3
    chips = 1 + max(i for i, _, _, _ in layout)
    bases = [((z ^ dz) * 4 + ((y + dy) & 3)) * 512 for dz, dy in where]
    slots, live = [], 0
    for i in range(chips):
        is_live = (bases[i] < plen).astype(jnp.int32)
        dead = i - live
        slots.append(jnp.where(is_live == 1, live, chips - 1 - dead))
        live = live + is_live
    steps = (live * 512 + CHUNK - 1) // CHUNK
    copies = []
    for n, (piece, (i, other, row, count)) in enumerate(zip(pieces, layout)):
        c = 1 - core if other else core
        to = pl.multiple_of(slots[i] * 512 + c * 256 + row, 128)
        for k, h in enumerate(heads):
            copy = pltpu.make_async_copy(
                piece.at[:, pl.ds(h * 256, 256)],
                kvs.at[k, pl.ds(to, count), :],
                sems.at[n * len(heads) + k],
            )
            copy.start()
            copies.append(copy)
    for i in range(chips):
        at = lax.broadcasted_iota(jnp.int32, (8, 512), 1) + bases[i]
        bias[slots[i]] = jnp.where(at < plen, 0.0, NEG)

    s_bufs, o_bufs = (sa, sb), (oa, ob)
    tiles = [(k, p) for k in range(len(heads)) for p in range(2)]

    def rows_of(p):
        return slice(p * ROWS, (p + 1) * ROWS)

    def begin1(n):
        k, p = tiles[n]
        if first:
            h = heads[k]
            s = nt(qs[k][rows_of(p), :], rkv[:, h * 256 : h * 256 + 128])
            key = lax.broadcasted_iota(jnp.int32, (ROWS, 256), 1)
            pos = p * 128 + lax.rem(lax.broadcasted_iota(jnp.int32, (ROWS, 256), 0), 128)
            s = jnp.where((key <= pos) & (key < rlen), s, NEG)
            o_bufs[n % 2][...] = s
            m_s[...] = jnp.maximum(s[:, :128], s[:, 128:])
        else:
            m_s[...] = states[k][0][rows_of(p), :]

    def pass1(n, c):
        k, p = tiles[n]
        keys = kvs[k, pl.ds(pl.multiple_of(c * CHUNK, CHUNK), CHUNK), 0:128]
        add = jnp.concatenate([bias[2 * c], bias[2 * c + 1]], axis=1)[0:1, :]
        s = nt(qs[k][rows_of(p), :], keys) + add
        s_bufs[n % 2][c] = s
        m_s[...] = lanes(s, jnp.maximum, m_s[...])

    def weigh(s, m):
        return jnp.concatenate(
            [
                jnp.exp2((s[:, i * 128 : (i + 1) * 128] - m) * LOG2E)
                for i in range(s.shape[1] // 128)
            ],
            axis=1,
        )

    def begin2(n):
        k, p = tiles[n]
        m = jnp.broadcast_to(jnp.max(m_s[...], axis=-1, keepdims=True), (ROWS, 128))
        mx_s[...] = m
        if first:
            h = heads[k]
            w = weigh(o_bufs[n % 2][...], m)
            l_s[...] = w[:, :128] + w[:, 128:]
            acc_s[...] = mm(w.astype(jnp.bfloat16), rkv[:, h * 256 + 128 : h * 256 + 256])
        else:
            old = jnp.exp2((states[k][0][rows_of(p), :] - m) * LOG2E)
            l_s[...] = states[k][1][rows_of(p), :] * old
            acc_s[...] = states[k][2][rows_of(p), :] * old

    def pass2(n, c):
        k, _ = tiles[n]
        values = kvs[k, pl.ds(pl.multiple_of(c * CHUNK, CHUNK), CHUNK), 128:256]
        w = weigh(s_bufs[n % 2][c], mx_s[...])
        l_s[...] = lanes(w, jnp.add, l_s[...])
        acc_s[...] += mm(w.astype(jnp.bfloat16), values)

    def finish(n):
        k, p = tiles[n]
        if not last:
            for ref, x in zip(outs[k], (mx_s, l_s, acc_s)):
                ref[rows_of(p), :] = x[...]
            return
        total = jnp.sum(l_s[...], axis=-1, keepdims=True)
        res = acc_s[...] / total
        pos = p * 128 + lax.rem(lax.broadcasted_iota(jnp.int32, (ROWS, 128), 0), 128)
        res = jnp.where(pos < rlen, res, 0.0).astype(jnp.bfloat16)
        for half in range(2):
            d = lax.rem(p * 2 + half - t + 4, 4)
            for e in range(4):

                @pl.when(d == e)
                def _():
                    for j in range(8):
                        r = j * 128 + half * 64
                        outs[k][e][:, j * 128 : (j + 1) * 128] = res[r : r + 64]

    begin1(0)
    for copy in copies:
        copy.wait()

    def loop(f):
        lax.fori_loop(0, steps, lambda c, z: (f(c), z)[1], 0)

    loop(lambda c: pass1(0, c))
    for n in range(len(tiles)):
        begin2(n)
        if n + 1 < len(tiles):
            begin1(n + 1)

            def both(c):
                pass1(n + 1, c)
                pass2(n, c)

            loop(both)
        else:
            loop(lambda c: pass2(n, c))
        finish(n)


def attend(heads, first, last, layout, where, meta, qs, rkv, pieces, states):
    vmem = pl.BlockSpec(memory_space=pltpu.VMEM)
    anywhere = pl.BlockSpec(memory_space=pl.ANY)
    chips = 1 + max(i for i, _, _, _ in layout)
    state = jax.ShapeDtypeStruct((2048, 128), jnp.float32)
    if last:
        out_shape = [jax.ShapeDtypeStruct((64, 1024), jnp.bfloat16)] * (4 * len(heads))
    else:
        out_shape = [state] * (3 * len(heads))
    steps = chips * 512 // CHUNK
    f32 = jnp.float32
    scratch = [
        pltpu.VMEM((len(heads), chips * 512, 256), jnp.bfloat16),
        pltpu.VMEM((chips, 8, 512), f32),
        *[pltpu.VMEM((ROWS, 128), f32)] * 4,
        *[pltpu.VMEM((steps, ROWS, CHUNK), f32)] * 2,
        *[pltpu.VMEM((ROWS if first else 8, 256), f32)] * 2,
        pltpu.SemaphoreType.DMA((len(layout) * len(heads),)),
    ]
    args = [meta, *qs] + ([rkv] if first else []) + list(pieces)
    specs = [pl.BlockSpec(memory_space=pltpu.SMEM)] + [vmem] * len(qs)
    specs += ([vmem] if first else []) + [anywhere] * len(pieces)
    if not first:
        args += [x for s in states for x in s]
        specs += [vmem] * (3 * len(heads))
    keys = chips * 512 + (256 if first else 0)
    return pl.pallas_call(
        functools.partial(attend_kernel, heads, first, last, layout, where),
        out_shape=tuple(out_shape),
        in_specs=specs,
        out_specs=(vmem,) * len(out_shape),
        scratch_shapes=scratch,
        compiler_params=pltpu.CompilerParams(vmem_limit_bytes=32 * MIB),
        name="attend",
    )(*args)


def gather_kernel(meta, *refs):
    pieces, out = refs[:8], refs[8]
    t = meta[2]
    for n, piece in enumerate(pieces):
        h, d = n // 4, n % 4
        to = pl.multiple_of(lax.rem(t - d + 4, 4) * 2048 + h * 1024, 1024)
        out[:, pl.ds(to, 1024)] = piece[...]


def assemble(meta, pieces):
    vmem = pl.BlockSpec(memory_space=pltpu.VMEM)
    return pl.pallas_call(
        gather_kernel,
        out_shape=jax.ShapeDtypeStruct((64, 8192), jnp.bfloat16),
        in_specs=[pl.BlockSpec(memory_space=pltpu.SMEM)] + [vmem] * 8,
        out_specs=vmem,
        compiler_params=pltpu.CompilerParams(vmem_limit_bytes=16 * MIB),
        name="assemble",
    )(meta, *pieces)


def place(z, y, c):
    return z * 8 + y * 2 + c


def move(x, dz, dy, dc=0):
    pairs = [
        (place(z, y, c), place(z ^ dz, (y + dy) % 4, c ^ dc))
        for z in range(2)
        for y in range(4)
        for c in range(2)
    ]
    return lax.ppermute(x, "resp", pairs)


def shift(x, d):
    return lax.ppermute(x, "tensor", [(i, (i + d) % 4) for i in range(4)])


def per_device(pk, pv, queries, rk, rv, q_gain, k_gain, prompt_len, resp_len):
    plen, rlen = prompt_len[0], resp_len[0]
    t = lax.axis_index("tensor")
    meta = jnp.stack([plen, rlen, t, lax.axis_index("resp")]).astype(jnp.int32)

    *mine, kv = split(meta, pk, pv, queries, rk, rv)
    q_pieces = [mine[0]] + [shift(mine[d], d) for d in (1, 2, 3)]
    kz, ka = move(kv, 1, 0), move(kv, 0, 1)
    kv, kz = lax.optimization_barrier((kv, kz))
    kb, ks = move(kv, 0, 3), move(kv, 0, 2)
    kza, kzb, kzs = move(kz, 0, 1), move(kz, 0, 3), move(kz, 0, 2)

    half = HEAD // 2
    pos = (plen + jnp.arange(LENGTH, dtype=jnp.int32)).astype(jnp.float32)
    freqs = jnp.power(
        jnp.float32(1000000.0), -jnp.arange(half).astype(jnp.float32) * (2.0 / HEAD)
    )
    angles = pos[:, None] * freqs[None, :]
    cosine, sine = jnp.cos(angles), jnp.sin(angles)
    c2 = jnp.concatenate([cosine, cosine], axis=1)
    s2 = jnp.concatenate([-sine, sine], axis=1)
    scale = HEAD ** (-0.5)
    tables = (
        c2 * (q_gain * scale),
        s2 * (jnp.roll(q_gain, half) * scale),
        c2 * k_gain,
        s2 * jnp.roll(k_gain, half),
    )
    q0, q1, rkv = prep(meta, q_pieces, tables)

    def both(pieces):
        return list(pieces) + [move(x, 0, 0, 1) for x in pieces]

    layout = [(i, o, 0, 256) for o in range(2) for i in range(4)]
    own_set, q_pieces[3] = lax.optimization_barrier(((kv, kz, ka, kb), q_pieces[3]))
    one = both(own_set)
    where_one = ((0, 0), (1, 0), (0, 3), (0, 1))
    where_two = ((1, 3), (1, 1), (0, 2), (1, 2))
    st0 = attend((0,), True, False, layout, where_one, meta, (q0,), rkv, one, None)
    (kza, kzb, ks, kzs), st0 = lax.optimization_barrier(((kza, kzb, ks, kzs), st0))
    two = both([kza, kzb, ks, kzs])
    st1 = attend((1,), True, False, layout, where_one, meta, (q1,), rkv, one, None)
    pieces = []
    for h, q, st in ((0, q0, st0), (1, q1, st1)):
        o = attend((h,), False, True, layout, where_two, meta, (q,), None, two, [st])
        pieces += [o[0]] + [shift(o[d], d) for d in (1, 2, 3)]
    return assemble(meta, pieces)


def solution(mesh):
    rows = P(("group", "resp", "tensor"), None)
    cache = P(("group", "resp"), "tensor")
    in_specs = (cache, cache, rows, rows, rows, P(), P(), P("group"), P(("group", "resp")))
    return jax.shard_map(
        per_device, mesh=mesh, in_specs=in_specs, out_specs=rows, check_vma=False
    )
```

```python
import functools

import jax
import jax.numpy as jnp
from jax import lax
from jax.experimental import pallas as pl
from jax.experimental.pallas import tpu as pltpu
from jax.sharding import PartitionSpec as P

HEAD = 128
LENGTH = 256
ROWS = 1024
CHUNK = 1024
LOG2E = 1.4426950408889634
NEG = -1e30
MIB = 1024 * 1024


def nt(a, b):
    return lax.dot_general(a, b, (((1,), (1,)), ((), ())), preferred_element_type=jnp.float32)


def mm(a, b):
    return jnp.dot(a, b, preferred_element_type=jnp.float32)


def split_kernel(meta, pk, pv, queries, rk, rv, *refs):
    q, kv = refs[:8], refs[8]
    t = meta[2]
    for h in range(2):
        for d in range(4):
            u = lax.rem(t + d, 4)
            dst = q[h * 4 + d]
            narrow = pl.ds(pl.multiple_of(u * 256 + h * 128, 128), 128)
            dst[:, :1024] = queries[:, pl.ds(pl.multiple_of(u * 2048 + h * 1024, 1024), 1024)]
            dst[:, 1024:1152] = rk[:, narrow]
            dst[:, 1152:] = rv[:, narrow]
        kv[:, h * 256 : h * 256 + 128] = pk[:, h * 128 : (h + 1) * 128]
        kv[:, h * 256 + 128 : h * 256 + 256] = pv[:, h * 128 : (h + 1) * 128]


def split(meta, *args):
    vmem = pl.BlockSpec(memory_space=pltpu.VMEM)
    piece = jax.ShapeDtypeStruct((64, 1280), jnp.bfloat16)
    return pl.pallas_call(
        split_kernel,
        out_shape=(piece,) * 8 + (jax.ShapeDtypeStruct((256, 512), jnp.bfloat16),),
        in_specs=[pl.BlockSpec(memory_space=pltpu.SMEM)] + [vmem] * 5,
        out_specs=(vmem,) * 9,
        compiler_params=pltpu.CompilerParams(vmem_limit_bytes=54 * MIB),
        name="split",
    )(meta, *args)


def prep_kernel(meta, own, r1, r2, r3, aq, bq, ak, bk, q, rkv):
    t = meta[2]
    wide = jnp.ones((256, 128), jnp.bfloat16)
    at = lax.broadcasted_iota(jnp.int32, (128, 128), 0)
    to = lax.broadcasted_iota(jnp.int32, (128, 128), 1)
    swap = jnp.where((at - to == 64) | (to - at == 64), 1.0, 0.0).astype(jnp.bfloat16)

    def rotated(x, a, b):
        f = x.astype(jnp.float32)
        sq = f * f
        hi = sq.astype(jnp.bfloat16)
        lo = (sq - hi.astype(jnp.float32)).astype(jnp.bfloat16)
        total = mm(jnp.concatenate([hi, lo], axis=1), wide)
        r = lax.rsqrt(total * (1.0 / HEAD) + 1e-06)
        return ((f * a + mm(x, swap) * b) * r).astype(jnp.bfloat16)

    for d, piece in enumerate((own, r1, r2, r3)):
        s = lax.rem(t - d + 4, 4)
        p0 = pl.multiple_of(s * 64, 64)
        rows = pl.ds(p0, 64)
        base = (s // 2) * ROWS + lax.rem(s, 2) * 64
        a8 = jnp.concatenate([aq[rows, :]] * 8, axis=0)
        b8 = jnp.concatenate([bq[rows, :]] * 8, axis=0)
        x = jnp.concatenate([piece[:, j * 128 : (j + 1) * 128] for j in range(8)], axis=0)
        y = rotated(x, a8, b8)
        for j in range(8):
            q[pl.ds(pl.multiple_of(base + j * 128, 64), 64), :] = y[j * 64 : (j + 1) * 64]
        rkv[rows, 0:128] = rotated(piece[:, 1024:1152], ak[rows, :], bk[rows, :])
        rkv[rows, 128:256] = piece[:, 1152:1280]


def prep(meta, pieces, tables):
    vmem = pl.BlockSpec(memory_space=pltpu.VMEM)
    return pl.pallas_call(
        prep_kernel,
        out_shape=(
            jax.ShapeDtypeStruct((2048, 128), jnp.bfloat16),
            jax.ShapeDtypeStruct((256, 256), jnp.bfloat16),
        ),
        in_specs=[pl.BlockSpec(memory_space=pltpu.SMEM)] + [vmem] * 8,
        out_specs=(vmem,) * 2,
        compiler_params=pltpu.CompilerParams(vmem_limit_bytes=16 * MIB),
        cost_estimate=pl.CostEstimate(flops=5 * 10**8, bytes_accessed=10**6, transcendentals=10**5),
        name="prep",
    )(meta, *pieces, *tables)


def lanes(x, f, start):
    for i in range(x.shape[1] // 128):
        start = f(start, x[:, i * 128 : (i + 1) * 128])
    return start


def attend_kernel(heads, first, last, layout, where, *refs):
    it = iter(refs)
    meta = next(it)
    qs = [next(it) for _ in heads]
    rkv = next(it) if first else None
    pieces = [next(it) for _ in layout]
    states = [[next(it) for _ in range(3)] for _ in heads] if not first else None
    outs = [[next(it) for _ in range(4)] if last else [next(it) for _ in range(3)] for _ in heads]
    kvs, bias, m_s, mx_s, l_s, acc_s, sa, sb, oa, ob, sems = it
    plen, rlen, t, r = meta[0], meta[1], meta[2], meta[3]
    core, y, z = r & 1, (r >> 1) & 3, r >> 3
    chips = 1 + max(i for i, _, _, _ in layout)
    bases = [((z ^ dz) * 4 + ((y + dy) & 3)) * 512 for dz, dy in where]
    slots, live = [], 0
    for i in range(chips):
        is_live = (bases[i] < plen).astype(jnp.int32)
        dead = i - live
        slots.append(jnp.where(is_live == 1, live, chips - 1 - dead))
        live = live + is_live
    steps = (live * 512 + CHUNK - 1) // CHUNK
    copies = []
    for n, (piece, (i, other, row, count)) in enumerate(zip(pieces, layout)):
        c = 1 - core if other else core
        to = pl.multiple_of(slots[i] * 512 + c * 256 + row, 128)
        for k, h in enumerate(heads):
            copy = pltpu.make_async_copy(
                piece.at[:, pl.ds(h * 256, 256)],
                kvs.at[k, pl.ds(to, count), :],
                sems.at[n * len(heads) + k],
            )
            copy.start()
            copies.append(copy)
    for i in range(chips):
        at = lax.broadcasted_iota(jnp.int32, (8, 512), 1) + bases[i]
        bias[slots[i]] = jnp.where(at < plen, 0.0, NEG)

    s_bufs, o_bufs = (sa, sb), (oa, ob)
    tiles = [(k, p) for k in range(len(heads)) for p in range(2)]

    def rows_of(p):
        return slice(p * ROWS, (p + 1) * ROWS)

    def begin1(n):
        k, p = tiles[n]
        if first:
            s = nt(qs[k][rows_of(p), :], rkv[:, :128])
            key = lax.broadcasted_iota(jnp.int32, (ROWS, 256), 1)
            pos = p * 128 + lax.rem(lax.broadcasted_iota(jnp.int32, (ROWS, 256), 0), 128)
            s = jnp.where((key <= pos) & (key < rlen), s, NEG)
            o_bufs[n % 2][...] = s
            m_s[...] = jnp.maximum(s[:, :128], s[:, 128:])
        else:
            m_s[...] = states[k][0][rows_of(p), :]

    def pass1(n, c):
        k, p = tiles[n]
        keys = kvs[k, pl.ds(pl.multiple_of(c * CHUNK, CHUNK), CHUNK), 0:128]
        add = jnp.concatenate([bias[2 * c], bias[2 * c + 1]], axis=1)[0:1, :]
        s = nt(qs[k][rows_of(p), :], keys) + add
        s_bufs[n % 2][c] = s
        m_s[...] = lanes(s, jnp.maximum, m_s[...])

    def weigh(s, m):
        return jnp.concatenate(
            [
                jnp.exp2((s[:, i * 128 : (i + 1) * 128] - m) * LOG2E)
                for i in range(s.shape[1] // 128)
            ],
            axis=1,
        )

    def begin2(n):
        k, p = tiles[n]
        m = jnp.broadcast_to(jnp.max(m_s[...], axis=-1, keepdims=True), (ROWS, 128))
        mx_s[...] = m
        if first:
            w = weigh(o_bufs[n % 2][...], m)
            l_s[...] = w[:, :128] + w[:, 128:]
            acc_s[...] = mm(w.astype(jnp.bfloat16), rkv[:, 128:])
        else:
            old = jnp.exp2((states[k][0][rows_of(p), :] - m) * LOG2E)
            l_s[...] = states[k][1][rows_of(p), :] * old
            acc_s[...] = states[k][2][rows_of(p), :] * old

    def pass2(n, c):
        k, _ = tiles[n]
        values = kvs[k, pl.ds(pl.multiple_of(c * CHUNK, CHUNK), CHUNK), 128:256]
        w = weigh(s_bufs[n % 2][c], mx_s[...])
        l_s[...] = lanes(w, jnp.add, l_s[...])
        acc_s[...] += mm(w.astype(jnp.bfloat16), values)

    def finish(n):
        k, p = tiles[n]
        if not last:
            for ref, x in zip(outs[k], (mx_s, l_s, acc_s)):
                ref[rows_of(p), :] = x[...]
            return
        total = jnp.sum(l_s[...], axis=-1, keepdims=True)
        res = acc_s[...] / total
        pos = p * 128 + lax.rem(lax.broadcasted_iota(jnp.int32, (ROWS, 128), 0), 128)
        res = jnp.where(pos < rlen, res, 0.0).astype(jnp.bfloat16)
        for half in range(2):
            d = lax.rem(p * 2 + half - t + 4, 4)
            for e in range(4):

                @pl.when(d == e)
                def _():
                    for j in range(8):
                        r = j * 128 + half * 64
                        outs[k][e][:, j * 128 : (j + 1) * 128] = res[r : r + 64]

    begin1(0)
    for copy in copies:
        copy.wait()

    def loop(f):
        lax.fori_loop(0, steps, lambda c, z: (f(c), z)[1], 0)

    loop(lambda c: pass1(0, c))
    for n in range(len(tiles)):
        begin2(n)
        if n + 1 < len(tiles):
            begin1(n + 1)

            def both(c):
                pass1(n + 1, c)
                pass2(n, c)

            loop(both)
        else:
            loop(lambda c: pass2(n, c))
        finish(n)


def attend(heads, first, last, layout, where, meta, qs, rkv, pieces, states, cost=8):
    vmem = pl.BlockSpec(memory_space=pltpu.VMEM)
    anywhere = pl.BlockSpec(memory_space=pl.ANY)
    chips = 1 + max(i for i, _, _, _ in layout)
    state = jax.ShapeDtypeStruct((2048, 128), jnp.float32)
    if last:
        out_shape = [jax.ShapeDtypeStruct((64, 1024), jnp.bfloat16)] * (4 * len(heads))
    else:
        out_shape = [state] * (3 * len(heads))
    steps = chips * 512 // CHUNK
    f32 = jnp.float32
    scratch = [
        pltpu.VMEM((len(heads), chips * 512, 256), jnp.bfloat16),
        pltpu.VMEM((chips, 8, 512), f32),
        *[pltpu.VMEM((ROWS, 128), f32)] * 4,
        *[pltpu.VMEM((steps, ROWS, CHUNK), f32)] * 2,
        *[pltpu.VMEM((ROWS if first else 8, 256), f32)] * 2,
        pltpu.SemaphoreType.DMA((len(layout) * len(heads),)),
    ]
    args = [meta, *qs] + ([rkv] if first else []) + list(pieces)
    specs = [pl.BlockSpec(memory_space=pltpu.SMEM)] + [vmem] * len(qs)
    specs += ([vmem] if first else []) + [anywhere] * len(pieces)
    if not first:
        args += [x for s in states for x in s]
        specs += [vmem] * (3 * len(heads))
    keys = chips * 512 + (256 if first else 0)
    return pl.pallas_call(
        functools.partial(attend_kernel, heads, first, last, layout, where),
        out_shape=tuple(out_shape),
        in_specs=specs,
        out_specs=(vmem,) * len(out_shape),
        scratch_shapes=scratch,
        compiler_params=pltpu.CompilerParams(vmem_limit_bytes=32 * MIB),
        cost_estimate=pl.CostEstimate(
            flops=cost * 2048 * keys * 128, bytes_accessed=4 * MIB, transcendentals=0
        ),
        name="attend",
    )(*args)


def gather_kernel(meta, *refs):
    pieces, out = refs[:8], refs[8]
    t = meta[2]
    for n, piece in enumerate(pieces):
        h, d = n // 4, n % 4
        to = pl.multiple_of(lax.rem(t - d + 4, 4) * 2048 + h * 1024, 1024)
        out[:, pl.ds(to, 1024)] = piece[...]


def assemble(meta, pieces):
    vmem = pl.BlockSpec(memory_space=pltpu.VMEM)
    return pl.pallas_call(
        gather_kernel,
        out_shape=jax.ShapeDtypeStruct((64, 8192), jnp.bfloat16),
        in_specs=[pl.BlockSpec(memory_space=pltpu.SMEM)] + [vmem] * 8,
        out_specs=vmem,
        compiler_params=pltpu.CompilerParams(vmem_limit_bytes=16 * MIB),
        name="assemble",
    )(meta, *pieces)


def place(z, y, c):
    return z * 8 + y * 2 + c


def move(x, dz, dy, dc=0):
    pairs = [
        (place(z, y, c), place(z ^ dz, (y + dy) % 4, c ^ dc))
        for z in range(2)
        for y in range(4)
        for c in range(2)
    ]
    return lax.ppermute(x, "resp", pairs)


def shift(x, d):
    return lax.ppermute(x, "tensor", [(i, (i + d) % 4) for i in range(4)])


def per_device(pk, pv, queries, rk, rv, q_gain, k_gain, prompt_len, resp_len):
    plen, rlen = prompt_len[0], resp_len[0]
    t = lax.axis_index("tensor")
    meta = jnp.stack([plen, rlen, t, lax.axis_index("resp")]).astype(jnp.int32)

    *mine, kv = split(meta, pk, pv, queries, rk, rv)
    kz, ka = move(kv, 1, 0), move(kv, 0, 1)
    q_of = [[mine[0]] + [shift(mine[d], d) for d in (1, 2, 3)]]
    kv, kz = lax.optimization_barrier((kv, kz))
    kb = move(kv, 0, 3)
    kv, ka = lax.optimization_barrier((kv, ka))
    ks = move(kv, 0, 2)
    other = [move(x, 0, 0, 1) for x in (kv, kz, ka)]
    mine, q_of[0], other = lax.optimization_barrier((mine, q_of[0], other))
    q_of.append([mine[4]] + [shift(mine[4 + d], d) for d in (1, 2, 3)])
    other.append(move(kb, 0, 0, 1))
    kz, other = lax.optimization_barrier((kz, other))
    kza, kzb = move(kz, 0, 1), move(kz, 0, 3)
    one = [kv, kz, ka, kb, *other]

    half = HEAD // 2
    pos = (plen + jnp.arange(LENGTH, dtype=jnp.int32)).astype(jnp.float32)
    freqs = jnp.power(
        jnp.float32(1000000.0), -jnp.arange(half).astype(jnp.float32) * (2.0 / HEAD)
    )
    angles = pos[:, None] * freqs[None, :]
    cosine, sine = jnp.cos(angles), jnp.sin(angles)
    c2 = jnp.concatenate([cosine, cosine], axis=1)
    s2 = jnp.concatenate([-sine, sine], axis=1)
    scale = HEAD ** (-0.5)
    tables = (
        c2 * (q_gain * scale),
        s2 * (jnp.roll(q_gain, half) * scale),
        c2 * k_gain,
        s2 * jnp.roll(k_gain, half),
    )
    q0, rkv0 = prep(meta, q_of[0], tables)

    def both(pieces):
        return list(pieces) + [move(x, 0, 0, 1) for x in pieces]

    layout = [(i, o, 0, 256) for o in range(2) for i in range(4)]
    where_one = ((0, 0), (1, 0), (0, 3), (0, 1))
    where_two = ((1, 3), (1, 1), (0, 2), (1, 2))
    st0 = attend((0,), True, False, layout, where_one, meta, (q0,), rkv0, one, None, 1)
    (kza, kzb, ks, kz, q_of[1]), st0 = lax.optimization_barrier(
        ((kza, kzb, ks, kz, q_of[1]), st0)
    )
    kzs = move(kz, 0, 2)
    q1, rkv1 = prep(meta, q_of[1], tables)
    two = both([kza, kzb, ks])
    st1 = attend((1,), True, False, layout, where_one, meta, (q1,), rkv1, one, None)
    kzs, st1 = lax.optimization_barrier((kzs, st1))
    two = [*two[:3], kzs, *two[3:], move(kzs, 0, 0, 1)]
    pieces = []
    for h, q, st in ((0, q0, st0), (1, q1, st1)):
        o = attend((h,), False, True, layout, where_two, meta, (q,), None, two, [st])
        pieces += [o[0]] + [shift(o[d], d) for d in (1, 2, 3)]
    return assemble(meta, pieces)


def solution(mesh):
    rows = P(("group", "resp", "tensor"), None)
    cache = P(("group", "resp"), "tensor")
    in_specs = (cache, cache, rows, rows, rows, P(), P(), P("group"), P(("group", "resp")))
    return jax.shard_map(
        per_device, mesh=mesh, in_specs=in_specs, out_specs=rows, check_vma=False
    )
```

```python
import functools

import jax
import jax.numpy as jnp
from jax import lax
from jax.experimental import pallas as pl
from jax.experimental.pallas import tpu as pltpu
from jax.sharding import PartitionSpec as P

HEAD = 128
LENGTH = 256
ROWS = 1024
CHUNK = 1024
LOG2E = 1.4426950408889634
NEG = -1e30
MIB = 1024 * 1024


def nt(a, b):
    return lax.dot_general(a, b, (((1,), (1,)), ((), ())), preferred_element_type=jnp.float32)


def mm(a, b):
    return jnp.dot(a, b, preferred_element_type=jnp.float32)


def split_kernel(pk, pv, queries, rk, rv, own, q1, q2, q3, kv0, kv1):
    t = lax.axis_index("tensor")
    for h, kv in enumerate((kv0, kv1)):
        kv[:, :128] = pk[:, h * 128 : (h + 1) * 128]
        kv[:, 128:] = pv[:, h * 128 : (h + 1) * 128]
    for d, dst in enumerate((own, q1, q2, q3)):
        u = lax.rem(t + d, 4)
        narrow = pl.ds(pl.multiple_of(u * 256, 256), 256)
        dst[:, :2048] = queries[:, pl.ds(pl.multiple_of(u * 2048, 2048), 2048)]
        dst[:, 2048:2304] = rk[:, narrow]
        dst[:, 2304:] = rv[:, narrow]


def split(*args):
    vmem = pl.BlockSpec(memory_space=pltpu.VMEM)
    piece = jax.ShapeDtypeStruct((64, 2560), jnp.bfloat16)
    cache = jax.ShapeDtypeStruct((256, 256), jnp.bfloat16)
    return pl.pallas_call(
        split_kernel,
        out_shape=(piece,) * 4 + (cache,) * 2,
        in_specs=[vmem] * 5,
        out_specs=(vmem,) * 6,
        compiler_params=pltpu.CompilerParams(vmem_limit_bytes=54 * MIB),
        name="split",
    )(*args)


def prep_kernel(own, r1, r2, r3, aq, bq, ak, bk, q0, q1, rkv0, rkv1):
    t = lax.axis_index("tensor")
    wide = jnp.ones((256, 128), jnp.bfloat16)
    at = lax.broadcasted_iota(jnp.int32, (128, 128), 0)
    to = lax.broadcasted_iota(jnp.int32, (128, 128), 1)
    swap = jnp.where((at - to == 64) | (to - at == 64), 1.0, 0.0).astype(jnp.bfloat16)

    def rotated(x, a, b):
        f = x.astype(jnp.float32)
        sq = f * f
        hi = sq.astype(jnp.bfloat16)
        lo = (sq - hi.astype(jnp.float32)).astype(jnp.bfloat16)
        total = mm(jnp.concatenate([hi, lo], axis=1), wide)
        r = lax.rsqrt(total * (1.0 / HEAD) + 1e-06)
        return ((f * a + mm(x, swap) * b) * r).astype(jnp.bfloat16)

    for d, piece in enumerate((own, r1, r2, r3)):
        s = lax.rem(t - d + 4, 4)
        p0 = pl.multiple_of(s * 64, 64)
        rows = pl.ds(p0, 64)
        base = (s // 2) * ROWS + lax.rem(s, 2) * 64
        a8 = jnp.concatenate([aq[rows, :]] * 8, axis=0)
        b8 = jnp.concatenate([bq[rows, :]] * 8, axis=0)
        for h, (q, rkv) in enumerate(((q0, rkv0), (q1, rkv1))):
            x = jnp.concatenate(
                [piece[:, (h * 8 + j) * 128 : (h * 8 + j + 1) * 128] for j in range(8)], axis=0
            )
            y = rotated(x, a8, b8)
            for j in range(8):
                q[pl.ds(pl.multiple_of(base + j * 128, 64), 64), :] = y[j * 64 : (j + 1) * 64]
            k = piece[:, 2048 + h * 128 : 2176 + h * 128]
            rkv[rows, 0:128] = rotated(k, ak[rows, :], bk[rows, :])
            rkv[rows, 128:256] = piece[:, 2304 + h * 128 : 2432 + h * 128]


def prep(pieces, tables):
    vmem = pl.BlockSpec(memory_space=pltpu.VMEM)
    q = jax.ShapeDtypeStruct((2048, 128), jnp.bfloat16)
    rkv = jax.ShapeDtypeStruct((256, 256), jnp.bfloat16)
    return pl.pallas_call(
        prep_kernel,
        out_shape=(q, q, rkv, rkv),
        in_specs=[vmem] * 8,
        out_specs=(vmem,) * 4,
        compiler_params=pltpu.CompilerParams(vmem_limit_bytes=16 * MIB),
        cost_estimate=pl.CostEstimate(flops=10**9, bytes_accessed=3 * 10**6, transcendentals=10**6),
        name="prep",
    )(*pieces, *tables)


def lanes(x, f, start):
    for i in range(x.shape[1] // 128):
        start = f(start, x[:, i * 128 : (i + 1) * 128])
    return start


def attend_kernel(where, plen_ref, rlen_ref, q, rkv, *refs):
    n_in = len(where) if where else 1
    pieces, outs = refs[:n_in], refs[n_in : n_in + 4]
    kvs, bias, m_s, mx_s, l_s, acc_s, sa, sb, oa, ob, sems = refs[n_in + 4 :]
    plen, rlen = plen_ref[0], rlen_ref[0]
    t, r = lax.axis_index("tensor"), lax.axis_index("resp")
    steps = (plen + CHUNK - 1) // CHUNK
    copies = []

    def copy(src, dst):
        copies.append(pltpu.make_async_copy(src, dst, sems.at[len(copies)]))
        copies[-1].start()

    if where:
        core, y, z = r & 1, (r >> 1) & 3, r >> 3
        for piece, (dy, other) in zip(pieces, where):
            for dz in range(2):
                to = ((z ^ dz) * 4 + ((y + dy) & 3)) * 512 + (core ^ other) * 256
                rows = pl.ds(pl.multiple_of(to, 256), 256)
                copy(piece.at[pl.ds(dz * 256, 256), :], kvs.at[rows, :])
    else:
        for c in range(4):
            rows = pl.ds(c * CHUNK, CHUNK)
            copy(pieces[0].at[rows, :], kvs.at[rows, :])
    for c in range(4):
        at = lax.broadcasted_iota(jnp.int32, (8, CHUNK), 1) + c * CHUNK
        bias[c] = jnp.where(at < plen, 0.0, NEG)

    s_bufs, o_bufs = (sa, sb), (oa, ob)

    def rows_of(p):
        return slice(p * ROWS, (p + 1) * ROWS)

    def chunk(c):
        return pl.ds(pl.multiple_of(c * CHUNK, CHUNK), CHUNK)

    def begin1(p):
        s = nt(q[rows_of(p), :], rkv[:, :128])
        key = lax.broadcasted_iota(jnp.int32, (ROWS, 256), 1)
        pos = p * 128 + lax.rem(lax.broadcasted_iota(jnp.int32, (ROWS, 256), 0), 128)
        s = jnp.where((key <= pos) & (key < rlen), s, NEG)
        o_bufs[p][...] = s
        m_s[...] = jnp.maximum(s[:, :128], s[:, 128:])

    def pass1(p, c):
        s = nt(q[rows_of(p), :], kvs[chunk(c), 0:128]) + bias[c][0:1, :]
        s_bufs[p][c] = s
        m_s[...] = lanes(s, jnp.maximum, m_s[...])

    def weigh(s, m):
        return jnp.concatenate(
            [
                jnp.exp2((s[:, i * 128 : (i + 1) * 128] - m) * LOG2E)
                for i in range(s.shape[1] // 128)
            ],
            axis=1,
        )

    def begin2(p):
        m = jnp.broadcast_to(jnp.max(m_s[...], axis=-1, keepdims=True), (ROWS, 128))
        mx_s[...] = m
        w = weigh(o_bufs[p][...], m)
        l_s[...] = w[:, :128] + w[:, 128:]
        acc_s[...] = mm(w.astype(jnp.bfloat16), rkv[:, 128:])

    def pass2(p, c):
        w = weigh(s_bufs[p][c], mx_s[...])
        l_s[...] = lanes(w, jnp.add, l_s[...])
        acc_s[...] += mm(w.astype(jnp.bfloat16), kvs[chunk(c), 128:256])

    def finish(p):
        total = jnp.sum(l_s[...], axis=-1, keepdims=True)
        res = acc_s[...] / total
        pos = p * 128 + lax.rem(lax.broadcasted_iota(jnp.int32, (ROWS, 128), 0), 128)
        res = jnp.where(pos < rlen, res, 0.0).astype(jnp.bfloat16)
        for half in range(2):
            d = lax.rem(p * 2 + half - t + 4, 4)
            for e in range(4):

                @pl.when(d == e)
                def _():
                    for j in range(8):
                        r0 = j * 128 + half * 64
                        outs[e][:, j * 128 : (j + 1) * 128] = res[r0 : r0 + 64]

    def loop(f):
        lax.fori_loop(0, steps, lambda c, x: (f(c), x)[1], 0)

    def both(c):
        pass1(1, c)
        pass2(0, c)

    begin1(0)
    for c in copies:
        c.wait()
    loop(lambda c: pass1(0, c))
    begin2(0)
    begin1(1)
    loop(both)
    finish(0)
    begin2(1)
    loop(lambda c: pass2(1, c))
    finish(1)


def attend(where, plen, rlen, q, rkv, pieces):
    vmem = pl.BlockSpec(memory_space=pltpu.VMEM)
    smem = pl.BlockSpec(memory_space=pltpu.SMEM)
    f32 = jnp.float32
    return pl.pallas_call(
        functools.partial(attend_kernel, where),
        out_shape=(jax.ShapeDtypeStruct((64, 1024), jnp.bfloat16),) * 4,
        in_specs=[smem] * 2 + [vmem] * 2 + [pl.BlockSpec(memory_space=pl.ANY)] * len(pieces),
        out_specs=(vmem,) * 4,
        scratch_shapes=[
            pltpu.VMEM((4096, 256), jnp.bfloat16),
            pltpu.VMEM((4, 8, CHUNK), f32),
            *[pltpu.VMEM((ROWS, 128), f32)] * 4,
            *[pltpu.VMEM((4, ROWS, CHUNK), f32)] * 2,
            *[pltpu.VMEM((ROWS, 256), f32)] * 2,
            pltpu.SemaphoreType.DMA((2 * len(pieces) if where else 4,)),
        ],
        compiler_params=pltpu.CompilerParams(vmem_limit_bytes=(46 if where else 52) * MIB),
        cost_estimate=pl.CostEstimate(
            flops=8 * 2048 * 4352 * 128, bytes_accessed=4 * MIB, transcendentals=2048 * 4352
        ),
        name="attend",
    )(plen, rlen, q, rkv, *pieces)


def gather_kernel(*refs):
    pieces, out = refs[:8], refs[8]
    t = lax.axis_index("tensor")
    for n, piece in enumerate(pieces):
        h, d = n // 4, n % 4
        to = pl.multiple_of(lax.rem(t - d + 4, 4) * 2048 + h * 1024, 1024)
        out[:, pl.ds(to, 1024)] = piece[...]


def assemble(pieces):
    vmem = pl.BlockSpec(memory_space=pltpu.VMEM)
    return pl.pallas_call(
        gather_kernel,
        out_shape=jax.ShapeDtypeStruct((64, 8192), jnp.bfloat16),
        in_specs=[vmem] * 8,
        out_specs=vmem,
        compiler_params=pltpu.CompilerParams(vmem_limit_bytes=16 * MIB),
        name="assemble",
    )(*pieces)


def place(z, y, c):
    return z * 8 + y * 2 + c


def move(x, dz, dy, dc=0):
    pairs = [
        (place(z, y, c), place(z ^ dz, (y + dy) % 4, c ^ dc))
        for z in range(2)
        for y in range(4)
        for c in range(2)
    ]
    return lax.ppermute(x, "resp", pairs)


def shift(x, d):
    return lax.ppermute(x, "tensor", [(i, (i + d) % 4) for i in range(4)])


def per_device(pk, pv, queries, rk, rv, q_gain, k_gain, prompt_len, resp_len):
    plen = prompt_len[0]
    *mine, kv0, kv1 = split(pk, pv, queries, rk, rv)
    all0 = lax.all_gather(kv0, "resp", axis=0, tiled=True)
    q_pieces = [mine[0]] + [shift(mine[d], d) for d in (1, 2, 3)]
    pair = jnp.concatenate([kv1, move(kv1, 1, 0)], axis=0)
    pairs = [pair] + [move(pair, 0, dy) for dy in (1, 3, 2)]
    pairs += [move(x, 0, 0, 1) for x in pairs]
    where = tuple((dy, other) for other in range(2) for dy in (0, 3, 1, 2))

    half = HEAD // 2
    pos = (plen + jnp.arange(LENGTH, dtype=jnp.int32)).astype(jnp.float32)
    freqs = jnp.power(
        jnp.float32(1000000.0), -jnp.arange(half).astype(jnp.float32) * (2.0 / HEAD)
    )
    angles = pos[:, None] * freqs[None, :]
    cosine, sine = jnp.cos(angles), jnp.sin(angles)
    c2 = jnp.concatenate([cosine, cosine], axis=1)
    s2 = jnp.concatenate([-sine, sine], axis=1)
    scale = HEAD ** (-0.5)
    tables = (
        c2 * (q_gain * scale),
        s2 * (jnp.roll(q_gain, half) * scale),
        c2 * k_gain,
        s2 * jnp.roll(k_gain, half),
    )
    q0, q1, rkv0, rkv1 = prep(q_pieces, tables)

    def send(o):
        return [o[0]] + [shift(o[d], d) for d in (1, 2, 3)]

    o1 = attend(where, prompt_len, resp_len, q1, rkv1, pairs)
    q0, own1 = lax.optimization_barrier((q0, o1[0]))
    sent1 = send((own1, *o1[1:]))
    o0 = attend(None, prompt_len, resp_len, q0, rkv0, [all0])
    return assemble(send(o0) + sent1)


def solution(mesh):
    rows = P(("group", "resp", "tensor"), None)
    cache = P(("group", "resp"), "tensor")
    in_specs = (cache, cache, rows, rows, rows, P(), P(), P("group"), P(("group", "resp")))
    return jax.shard_map(
        per_device, mesh=mesh, in_specs=in_specs, out_specs=rows, check_vma=False
    )
```

```python
import functools

import jax
import jax.numpy as jnp
from jax import lax
from jax.experimental import pallas as pl
from jax.experimental.pallas import tpu as pltpu
from jax.sharding import PartitionSpec as P

HEAD = 128
LENGTH = 256
ROWS = 1024
CHUNK = 1024
LOG2E = 1.4426950408889634
NEG = -1e30
MIB = 1024 * 1024


def nt(a, b):
    return lax.dot_general(a, b, (((1,), (1,)), ((), ())), preferred_element_type=jnp.float32)


def mm(a, b):
    return jnp.dot(a, b, preferred_element_type=jnp.float32)


def split_kernel(pk, pv, queries, rk, rv, own, q1, q2, q3, kv):
    t = lax.axis_index("tensor")
    for h in range(2):
        kv[:, h * 256 : h * 256 + 128] = pk[:, h * 128 : (h + 1) * 128]
        kv[:, h * 256 + 128 : h * 256 + 256] = pv[:, h * 128 : (h + 1) * 128]
    for d, dst in enumerate((own, q1, q2, q3)):
        u = lax.rem(t + d, 4)
        narrow = pl.ds(pl.multiple_of(u * 256, 256), 256)
        dst[:, :2048] = queries[:, pl.ds(pl.multiple_of(u * 2048, 2048), 2048)]
        dst[:, 2048:2304] = rk[:, narrow]
        dst[:, 2304:] = rv[:, narrow]


def split(*args):
    vmem = pl.BlockSpec(memory_space=pltpu.VMEM)
    piece = jax.ShapeDtypeStruct((64, 2560), jnp.bfloat16)
    cache = jax.ShapeDtypeStruct((256, 512), jnp.bfloat16)
    return pl.pallas_call(
        split_kernel,
        out_shape=(piece,) * 4 + (cache,),
        in_specs=[vmem] * 5,
        out_specs=(vmem,) * 5,
        compiler_params=pltpu.CompilerParams(vmem_limit_bytes=54 * MIB),
        name="split",
    )(*args)


def prep_kernel(own, r1, r2, r3, aq, bq, ak, bk, q0, q1, rkv0, rkv1):
    t = lax.axis_index("tensor")
    wide = jnp.ones((256, 128), jnp.bfloat16)
    at = lax.broadcasted_iota(jnp.int32, (128, 128), 0)
    to = lax.broadcasted_iota(jnp.int32, (128, 128), 1)
    swap = jnp.where((at - to == 64) | (to - at == 64), 1.0, 0.0).astype(jnp.bfloat16)

    def rotated(x, a, b):
        f = x.astype(jnp.float32)
        sq = f * f
        hi = sq.astype(jnp.bfloat16)
        lo = (sq - hi.astype(jnp.float32)).astype(jnp.bfloat16)
        total = mm(jnp.concatenate([hi, lo], axis=1), wide)
        r = lax.rsqrt(total * (1.0 / HEAD) + 1e-06)
        return ((f * a + mm(x, swap) * b) * r).astype(jnp.bfloat16)

    for d, piece in enumerate((own, r1, r2, r3)):
        s = lax.rem(t - d + 4, 4)
        p0 = pl.multiple_of(s * 64, 64)
        rows = pl.ds(p0, 64)
        base = (s // 2) * ROWS + lax.rem(s, 2) * 64
        a8 = jnp.concatenate([aq[rows, :]] * 8, axis=0)
        b8 = jnp.concatenate([bq[rows, :]] * 8, axis=0)
        for h, (q, rkv) in enumerate(((q0, rkv0), (q1, rkv1))):
            x = jnp.concatenate(
                [piece[:, (h * 8 + j) * 128 : (h * 8 + j + 1) * 128] for j in range(8)], axis=0
            )
            y = rotated(x, a8, b8)
            for j in range(8):
                q[pl.ds(pl.multiple_of(base + j * 128, 64), 64), :] = y[j * 64 : (j + 1) * 64]
            k = piece[:, 2048 + h * 128 : 2176 + h * 128]
            rkv[rows, 0:128] = rotated(k, ak[rows, :], bk[rows, :])
            rkv[rows, 128:256] = piece[:, 2304 + h * 128 : 2432 + h * 128]


def prep(pieces, tables):
    vmem = pl.BlockSpec(memory_space=pltpu.VMEM)
    q = jax.ShapeDtypeStruct((2048, 128), jnp.bfloat16)
    rkv = jax.ShapeDtypeStruct((256, 256), jnp.bfloat16)
    return pl.pallas_call(
        prep_kernel,
        out_shape=(q, q, rkv, rkv),
        in_specs=[vmem] * 8,
        out_specs=(vmem,) * 4,
        compiler_params=pltpu.CompilerParams(vmem_limit_bytes=16 * MIB),
        cost_estimate=pl.CostEstimate(flops=10**9, bytes_accessed=3 * 10**6, transcendentals=10**6),
        name="prep",
    )(*pieces, *tables)


def lanes(x, f, start):
    for i in range(x.shape[1] // 128):
        start = f(start, x[:, i * 128 : (i + 1) * 128])
    return start


def attend_kernel(heads, first, last, layout, where, *refs):
    it = iter(refs)
    plen_ref, rlen_ref = next(it), next(it)
    qs = [next(it) for _ in heads]
    rkvs = [next(it) for _ in heads] if first else None
    pieces = [next(it) for _ in range(1 + max(n for n, _, _, _ in layout))]
    states = [[next(it) for _ in range(3)] for _ in heads] if not first else None
    outs = [[next(it) for _ in range(4)] if last else [next(it) for _ in range(3)] for _ in heads]
    kvs, bias, m_s, mx_s, l_s, acc_s, sa, sb, oa, ob, sems = it
    plen, rlen = plen_ref[0], rlen_ref[0]
    t, r = lax.axis_index("tensor"), lax.axis_index("resp")
    core, y, z = r & 1, (r >> 1) & 3, r >> 3
    chips = len(where)
    bases = [((z ^ dz) * 4 + ((y + dy) & 3)) * 512 for dz, dy in where]
    slots, live = [], 0
    for i in range(chips):
        is_live = (bases[i] < plen).astype(jnp.int32)
        dead = i - live
        slots.append(jnp.where(is_live == 1, live, chips - 1 - dead))
        live = live + is_live
    steps = (live * 512 + CHUNK - 1) // CHUNK
    copies = []
    for m, (n, i, other, row) in enumerate(layout):
        c = 1 - core if other else core
        to = pl.multiple_of(slots[i] * 512 + c * 256, 256)
        for k, h in enumerate(heads):
            copy = pltpu.make_async_copy(
                pieces[n].at[pl.ds(row, 256), pl.ds(h * 256, 256)],
                kvs.at[k, pl.ds(to, 256), :],
                sems.at[m * len(heads) + k],
            )
            copy.start()
            copies.append(copy)
    for i in range(chips):
        at = lax.broadcasted_iota(jnp.int32, (8, 512), 1) + bases[i]
        bias[slots[i]] = jnp.where(at < plen, 0.0, NEG)

    s_bufs, o_bufs = (sa, sb), (oa, ob)
    tiles = [(k, p) for k in range(len(heads)) for p in range(2)]

    def rows_of(p):
        return slice(p * ROWS, (p + 1) * ROWS)

    def begin1(n):
        k, p = tiles[n]
        if first:
            s = nt(qs[k][rows_of(p), :], rkvs[k][:, :128])
            key = lax.broadcasted_iota(jnp.int32, (ROWS, 256), 1)
            pos = p * 128 + (lax.broadcasted_iota(jnp.int32, (ROWS, 256), 0) & 127)
            s = jnp.where((key <= pos) & (key < rlen), s, NEG)
            o_bufs[n % 2][...] = s
            m_s[...] = jnp.maximum(s[:, :128], s[:, 128:])
        else:
            m_s[...] = states[k][0][rows_of(p), :]

    def pass1(n, c):
        k, p = tiles[n]
        keys = kvs[k, pl.ds(pl.multiple_of(c * CHUNK, CHUNK), CHUNK), 0:128]
        add = jnp.concatenate([bias[2 * c], bias[2 * c + 1]], axis=1)[0:1, :]
        s = nt(qs[k][rows_of(p), :], keys) + add
        s_bufs[n % 2][c] = s
        m_s[...] = lanes(s, jnp.maximum, m_s[...])

    def weigh(s, m):
        return jnp.concatenate(
            [
                jnp.exp2((s[:, i * 128 : (i + 1) * 128] - m) * LOG2E)
                for i in range(s.shape[1] // 128)
            ],
            axis=1,
        )

    def begin2(n):
        k, p = tiles[n]
        m = jnp.broadcast_to(jnp.max(m_s[...], axis=-1, keepdims=True), (ROWS, 128))
        mx_s[...] = m
        if first:
            w = weigh(o_bufs[n % 2][...], m)
            l_s[...] = w[:, :128] + w[:, 128:]
            acc_s[...] = mm(w.astype(jnp.bfloat16), rkvs[k][:, 128:])
        else:
            old = jnp.exp2((states[k][0][rows_of(p), :] - m) * LOG2E)
            l_s[...] = states[k][1][rows_of(p), :] * old
            acc_s[...] = states[k][2][rows_of(p), :] * old

    def pass2(n, c):
        k, _ = tiles[n]
        values = kvs[k, pl.ds(pl.multiple_of(c * CHUNK, CHUNK), CHUNK), 128:256]
        w = weigh(s_bufs[n % 2][c], mx_s[...])
        l_s[...] = lanes(w, jnp.add, l_s[...])
        acc_s[...] += mm(w.astype(jnp.bfloat16), values)

    def finish(n):
        k, p = tiles[n]
        if not last:
            for ref, x in zip(outs[k], (mx_s, l_s, acc_s)):
                ref[rows_of(p), :] = x[...]
            return
        total = jnp.sum(l_s[...], axis=-1, keepdims=True)
        res = acc_s[...] / total
        pos = p * 128 + (lax.broadcasted_iota(jnp.int32, (ROWS, 128), 0) & 127)
        res = jnp.where(pos < rlen, res, 0.0).astype(jnp.bfloat16)
        for half in range(2):
            d = lax.rem(p * 2 + half - t + 4, 4)
            for e in range(4):

                @pl.when(d == e)
                def _():
                    for j in range(8):
                        r = j * 128 + half * 64
                        outs[k][e][:, j * 128 : (j + 1) * 128] = res[r : r + 64]

    begin1(0)
    for copy in copies:
        copy.wait()

    def loop(f):
        lax.fori_loop(0, steps, lambda c, z: (f(c), z)[1], 0)

    loop(lambda c: pass1(0, c))
    for n in range(len(tiles)):
        begin2(n)
        if n + 1 < len(tiles):
            begin1(n + 1)

            def both(c):
                pass1(n + 1, c)
                pass2(n, c)

            loop(both)
        else:
            loop(lambda c: pass2(n, c))
        finish(n)


def attend(heads, first, last, layout, where, lens, qs, rkvs, pieces, states):
    vmem = pl.BlockSpec(memory_space=pltpu.VMEM)
    anywhere = pl.BlockSpec(memory_space=pl.ANY)
    chips = len(where)
    state = jax.ShapeDtypeStruct((2048, 128), jnp.float32)
    if last:
        out_shape = [jax.ShapeDtypeStruct((64, 1024), jnp.bfloat16)] * (4 * len(heads))
    else:
        out_shape = [state] * (3 * len(heads))
    steps = chips * 512 // CHUNK
    f32 = jnp.float32
    scratch = [
        pltpu.VMEM((len(heads), chips * 512, 256), jnp.bfloat16),
        pltpu.VMEM((chips, 8, 512), f32),
        *[pltpu.VMEM((ROWS, 128), f32)] * 4,
        *[pltpu.VMEM((steps, ROWS, CHUNK), f32)] * 2,
        *[pltpu.VMEM((ROWS if first else 8, 256), f32)] * 2,
        pltpu.SemaphoreType.DMA((len(layout) * len(heads),)),
    ]
    args = [*lens, *qs] + (list(rkvs) if first else []) + list(pieces)
    specs = [pl.BlockSpec(memory_space=pltpu.SMEM)] * 2 + [vmem] * len(qs)
    specs += ([vmem] * len(qs) if first else []) + [anywhere] * len(pieces)
    if not first:
        args += [x for s in states for x in s]
        specs += [vmem] * (3 * len(heads))
    keys = chips * 512 + (256 if first else 0)
    return pl.pallas_call(
        functools.partial(attend_kernel, heads, first, last, layout, where),
        out_shape=tuple(out_shape),
        in_specs=specs,
        out_specs=(vmem,) * len(out_shape),
        scratch_shapes=scratch,
        compiler_params=pltpu.CompilerParams(vmem_limit_bytes=40 * MIB),
        cost_estimate=pl.CostEstimate(
            flops=8 * 2048 * keys * 128 * len(heads),
            bytes_accessed=4 * MIB,
            transcendentals=2048 * keys * len(heads),
        ),
        name="attend",
    )(*args)


def gather_kernel(*refs):
    pieces, out = refs[:8], refs[8]
    t = lax.axis_index("tensor")
    for n, piece in enumerate(pieces):
        h, d = n // 4, n % 4
        to = pl.multiple_of(lax.rem(t - d + 4, 4) * 2048 + h * 1024, 1024)
        out[:, pl.ds(to, 1024)] = piece[...]


def assemble(pieces):
    vmem = pl.BlockSpec(memory_space=pltpu.VMEM)
    return pl.pallas_call(
        gather_kernel,
        out_shape=jax.ShapeDtypeStruct((64, 8192), jnp.bfloat16),
        in_specs=[vmem] * 8,
        out_specs=vmem,
        compiler_params=pltpu.CompilerParams(vmem_limit_bytes=16 * MIB),
        name="assemble",
    )(*pieces)


def place(z, y, c):
    return z * 8 + y * 2 + c


def move(x, dz, dy, dc=0):
    pairs = [
        (place(z, y, c), place(z ^ dz, (y + dy) % 4, c ^ dc))
        for z in range(2)
        for y in range(4)
        for c in range(2)
    ]
    return lax.ppermute(x, "resp", pairs)


def shift(x, d):
    return lax.ppermute(x, "tensor", [(i, (i + d) % 4) for i in range(4)])


def per_device(pk, pv, queries, rk, rv, q_gain, k_gain, prompt_len, resp_len):
    plen = prompt_len[0]
    *mine, kv = split(pk, pv, queries, rk, rv)
    q_pieces = [mine[0]] + [shift(mine[d], d) for d in (1, 2, 3)]
    pair = jnp.concatenate([kv, move(kv, 1, 0)], axis=0)
    near, away, opposite = (move(pair, 0, dy) for dy in (1, 3, 2))

    half = HEAD // 2
    pos = (plen + jnp.arange(LENGTH, dtype=jnp.int32)).astype(jnp.float32)
    freqs = jnp.power(
        jnp.float32(1000000.0), -jnp.arange(half).astype(jnp.float32) * (2.0 / HEAD)
    )
    angles = pos[:, None] * freqs[None, :]
    cosine, sine = jnp.cos(angles), jnp.sin(angles)
    c2 = jnp.concatenate([cosine, cosine], axis=1)
    s2 = jnp.concatenate([-sine, sine], axis=1)
    scale = HEAD ** (-0.5)
    tables = (
        c2 * (q_gain * scale),
        s2 * (jnp.roll(q_gain, half) * scale),
        c2 * k_gain,
        s2 * jnp.roll(k_gain, half),
    )
    q0, q1, rkv0, rkv1 = prep(q_pieces, tables)

    def send(o):
        return [o[0]] + [shift(o[d], d) for d in (1, 2, 3)]

    def both(pieces):
        return list(pieces) + [move(x, 0, 0, 1) for x in pieces]

    lens = (prompt_len, resp_len)
    layout = tuple((o, z, o, z * 256) for o in range(2) for z in range(2))
    st = attend(
        (0, 1),
        True,
        False,
        layout,
        ((0, 0), (1, 0)),
        lens,
        (q0, q1),
        (rkv0, rkv1),
        both([pair]),
        None,
    )
    rest, st = lax.optimization_barrier(((near, away, opposite), st))
    rest = both(rest)
    where = tuple((z, dy) for dy in (3, 1, 2) for z in range(2))
    layout = tuple(
        (o * 3 + n, n * 2 + z, o, z * 256) for o in range(2) for n in range(3) for z in range(2)
    )
    pieces = []
    for h, q in enumerate((q0, q1)):
        states = [st[3 * h : 3 * h + 3]]
        pieces += send(attend((h,), False, True, layout, where, lens, (q,), None, rest, states))
    return assemble(pieces)


def solution(mesh):
    rows = P(("group", "resp", "tensor"), None)
    cache = P(("group", "resp"), "tensor")
    in_specs = (cache, cache, rows, rows, rows, P(), P(), P("group"), P(("group", "resp")))
    return jax.shard_map(
        per_device, mesh=mesh, in_specs=in_specs, out_specs=rows, check_vma=False
    )
```

```python
import functools

import jax
import jax.numpy as jnp
from jax import lax
from jax.experimental import pallas as pl
from jax.experimental.pallas import tpu as pltpu
from jax.sharding import PartitionSpec as P

HEAD = 128
LENGTH = 256
ROWS = 1024
CHUNK = 1024
LOG2E = 1.4426950408889634
NEG = -1e30
MIB = 1024 * 1024


def nt(a, b):
    return lax.dot_general(a, b, (((1,), (1,)), ((), ())), preferred_element_type=jnp.float32)


def mm(a, b):
    return jnp.dot(a, b, preferred_element_type=jnp.float32)


def split_kernel(pk, pv, queries, rk, rv, own, q1, q2, q3, kv):
    t = lax.axis_index("tensor")
    for h in range(2):
        kv[:, h * 256 : h * 256 + 128] = pk[:, h * 128 : (h + 1) * 128]
        kv[:, h * 256 + 128 : h * 256 + 256] = pv[:, h * 128 : (h + 1) * 128]
    for d, dst in enumerate((own, q1, q2, q3)):
        u = lax.rem(t + d, 4)
        narrow = pl.ds(pl.multiple_of(u * 256, 256), 256)
        dst[:, :2048] = queries[:, pl.ds(pl.multiple_of(u * 2048, 2048), 2048)]
        dst[:, 2048:2304] = rk[:, narrow]
        dst[:, 2304:] = rv[:, narrow]


def split(*args):
    vmem = pl.BlockSpec(memory_space=pltpu.VMEM)
    piece = jax.ShapeDtypeStruct((64, 2560), jnp.bfloat16)
    cache = jax.ShapeDtypeStruct((256, 512), jnp.bfloat16)
    return pl.pallas_call(
        split_kernel,
        out_shape=(piece,) * 4 + (cache,),
        in_specs=[vmem] * 5,
        out_specs=(vmem,) * 5,
        compiler_params=pltpu.CompilerParams(vmem_limit_bytes=54 * MIB),
        name="split",
    )(*args)


def prep_kernel(own, r1, r2, r3, aq, bq, ak, bk, q0, q1, rkv0, rkv1):
    t = lax.axis_index("tensor")
    wide = jnp.ones((256, 128), jnp.bfloat16)
    at = lax.broadcasted_iota(jnp.int32, (128, 128), 0)
    to = lax.broadcasted_iota(jnp.int32, (128, 128), 1)
    swap = jnp.where((at - to == 64) | (to - at == 64), 1.0, 0.0).astype(jnp.bfloat16)

    def rotated(x, a, b):
        f = x.astype(jnp.float32)
        sq = f * f
        hi = sq.astype(jnp.bfloat16)
        lo = (sq - hi.astype(jnp.float32)).astype(jnp.bfloat16)
        total = mm(jnp.concatenate([hi, lo], axis=1), wide)
        r = lax.rsqrt(total * (1.0 / HEAD) + 1e-06)
        return ((f * a + mm(x, swap) * b) * r).astype(jnp.bfloat16)

    for d, piece in enumerate((own, r1, r2, r3)):
        s = lax.rem(t - d + 4, 4)
        p0 = pl.multiple_of(s * 64, 64)
        rows = pl.ds(p0, 64)
        base = (s // 2) * ROWS + lax.rem(s, 2) * 64
        a8 = jnp.concatenate([aq[rows, :]] * 8, axis=0)
        b8 = jnp.concatenate([bq[rows, :]] * 8, axis=0)
        for h, (q, rkv) in enumerate(((q0, rkv0), (q1, rkv1))):
            x = jnp.concatenate(
                [piece[:, (h * 8 + j) * 128 : (h * 8 + j + 1) * 128] for j in range(8)], axis=0
            )
            y = rotated(x, a8, b8)
            for j in range(8):
                q[pl.ds(pl.multiple_of(base + j * 128, 64), 64), :] = y[j * 64 : (j + 1) * 64]
            k = piece[:, 2048 + h * 128 : 2176 + h * 128]
            rkv[rows, 0:128] = rotated(k, ak[rows, :], bk[rows, :])
            rkv[rows, 128:256] = piece[:, 2304 + h * 128 : 2432 + h * 128]


def prep(pieces, tables):
    vmem = pl.BlockSpec(memory_space=pltpu.VMEM)
    q = jax.ShapeDtypeStruct((2048, 128), jnp.bfloat16)
    rkv = jax.ShapeDtypeStruct((256, 256), jnp.bfloat16)
    return pl.pallas_call(
        prep_kernel,
        out_shape=(q, q, rkv, rkv),
        in_specs=[vmem] * 8,
        out_specs=(vmem,) * 4,
        compiler_params=pltpu.CompilerParams(vmem_limit_bytes=16 * MIB),
        cost_estimate=pl.CostEstimate(flops=10**9, bytes_accessed=3 * 10**6, transcendentals=10**6),
        name="prep",
    )(*pieces, *tables)


def lanes(x, f, start):
    for i in range(x.shape[1] // 128):
        start = f(start, x[:, i * 128 : (i + 1) * 128])
    return start


def attend_kernel(heads, first, last, layout, where, *refs):
    it = iter(refs)
    plen_ref, rlen_ref = next(it), next(it)
    qs = [next(it) for _ in heads]
    rkvs = [next(it) for _ in heads] if first else None
    pieces = [next(it) for _ in range(1 + max(n for n, _, _, _ in layout))]
    states = [[next(it) for _ in range(3)] for _ in heads] if not first else None
    outs = [[next(it) for _ in range(4)] if last else [next(it) for _ in range(3)] for _ in heads]
    kvs, bias, m_s, mx_s, l_s, acc_s, sa, sb, oa, ob, sems = it
    plen, rlen = plen_ref[0], rlen_ref[0]
    t, r = lax.axis_index("tensor"), lax.axis_index("resp")
    core, y, z = r & 1, (r >> 1) & 3, r >> 3
    chips = len(where)
    bases = [((z ^ dz) * 4 + ((y + dy) & 3)) * 512 for dz, dy in where]
    slots, live = [], 0
    for i in range(chips):
        is_live = (bases[i] < plen).astype(jnp.int32)
        dead = i - live
        slots.append(jnp.where(is_live == 1, live, chips - 1 - dead))
        live = live + is_live
    steps = (live * 512 + CHUNK - 1) // CHUNK
    copies = []
    for m, (n, i, other, row) in enumerate(layout):
        c = 1 - core if other else core
        to = pl.multiple_of(slots[i] * 512 + c * 256, 256)
        for k, h in enumerate(heads):
            copy = pltpu.make_async_copy(
                pieces[n].at[pl.ds(row, 256), pl.ds(h * 256, 256)],
                kvs.at[k, pl.ds(to, 256), :],
                sems.at[m * len(heads) + k],
            )
            copy.start()
            copies.append(copy)
    for i in range(chips):
        at = lax.broadcasted_iota(jnp.int32, (8, 512), 1) + bases[i]
        bias[slots[i]] = jnp.where(at < plen, 0.0, NEG)

    s_bufs, o_bufs = (sa, sb), (oa, ob)
    tiles = [(k, p) for k in range(len(heads)) for p in range(2)]

    def rows_of(p):
        return slice(p * ROWS, (p + 1) * ROWS)

    def begin1(n):
        k, p = tiles[n]
        if first:
            s = nt(qs[k][rows_of(p), :], rkvs[k][:, :128])
            key = lax.broadcasted_iota(jnp.int32, (ROWS, 256), 1)
            pos = p * 128 + (lax.broadcasted_iota(jnp.int32, (ROWS, 256), 0) & 127)
            s = jnp.where((key <= pos) & (key < rlen), s, NEG)
            o_bufs[n % 2][...] = s
            m_s[...] = jnp.maximum(s[:, :128], s[:, 128:])
        else:
            m_s[...] = states[k][0][rows_of(p), :]

    def pass1(n, c):
        k, p = tiles[n]
        keys = kvs[k, pl.ds(pl.multiple_of(c * CHUNK, CHUNK), CHUNK), 0:128]
        add = jnp.concatenate([bias[2 * c], bias[2 * c + 1]], axis=1)[0:1, :]
        s = nt(qs[k][rows_of(p), :], keys) + add
        s_bufs[n % 2][c] = s
        m_s[...] = lanes(s, jnp.maximum, m_s[...])

    def weigh(s, m):
        return jnp.concatenate(
            [
                jnp.exp2((s[:, i * 128 : (i + 1) * 128] - m) * LOG2E)
                for i in range(s.shape[1] // 128)
            ],
            axis=1,
        )

    def begin2(n):
        k, p = tiles[n]
        m = jnp.broadcast_to(jnp.max(m_s[...], axis=-1, keepdims=True), (ROWS, 128))
        mx_s[...] = m
        if first:
            w = weigh(o_bufs[n % 2][...], m)
            l_s[...] = w[:, :128] + w[:, 128:]
            acc_s[...] = mm(w.astype(jnp.bfloat16), rkvs[k][:, 128:])
        else:
            old = jnp.exp2((states[k][0][rows_of(p), :] - m) * LOG2E)
            l_s[...] = states[k][1][rows_of(p), :] * old
            acc_s[...] = states[k][2][rows_of(p), :] * old

    def pass2(n, c):
        k, _ = tiles[n]
        values = kvs[k, pl.ds(pl.multiple_of(c * CHUNK, CHUNK), CHUNK), 128:256]
        w = weigh(s_bufs[n % 2][c], mx_s[...])
        l_s[...] = lanes(w, jnp.add, l_s[...])
        acc_s[...] += mm(w.astype(jnp.bfloat16), values)

    def finish(n):
        k, p = tiles[n]
        if not last:
            for ref, x in zip(outs[k], (mx_s, l_s, acc_s)):
                ref[rows_of(p), :] = x[...]
            return
        total = jnp.sum(l_s[...], axis=-1, keepdims=True)
        res = acc_s[...] / total
        pos = p * 128 + (lax.broadcasted_iota(jnp.int32, (ROWS, 128), 0) & 127)
        res = jnp.where(pos < rlen, res, 0.0).astype(jnp.bfloat16)
        for half in range(2):
            d = lax.rem(p * 2 + half - t + 4, 4)
            for e in range(4):

                @pl.when(d == e)
                def _():
                    for j in range(8):
                        r = j * 128 + half * 64
                        outs[k][e][:, j * 128 : (j + 1) * 128] = res[r : r + 64]

    begin1(0)
    for copy in copies:
        copy.wait()

    def loop(f):
        lax.fori_loop(0, steps, lambda c, z: (f(c), z)[1], 0)

    loop(lambda c: pass1(0, c))
    for n in range(len(tiles)):
        begin2(n)
        if n + 1 < len(tiles):
            begin1(n + 1)

            def both(c):
                pass1(n + 1, c)
                pass2(n, c)

            loop(both)
        else:
            loop(lambda c: pass2(n, c))
        finish(n)


def attend(heads, first, last, layout, where, lens, qs, rkvs, pieces, states):
    vmem = pl.BlockSpec(memory_space=pltpu.VMEM)
    anywhere = pl.BlockSpec(memory_space=pl.ANY)
    chips = len(where)
    state = jax.ShapeDtypeStruct((2048, 128), jnp.float32)
    if last:
        out_shape = [jax.ShapeDtypeStruct((64, 1024), jnp.bfloat16)] * (4 * len(heads))
    else:
        out_shape = [state] * (3 * len(heads))
    steps = chips * 512 // CHUNK
    f32 = jnp.float32
    scratch = [
        pltpu.VMEM((len(heads), chips * 512, 256), jnp.bfloat16),
        pltpu.VMEM((chips, 8, 512), f32),
        *[pltpu.VMEM((ROWS, 128), f32)] * 4,
        *[pltpu.VMEM((steps, ROWS, CHUNK), f32)] * 2,
        *[pltpu.VMEM((ROWS if first else 8, 256), f32)] * 2,
        pltpu.SemaphoreType.DMA((len(layout) * len(heads),)),
    ]
    args = [*lens, *qs] + (list(rkvs) if first else []) + list(pieces)
    specs = [pl.BlockSpec(memory_space=pltpu.SMEM)] * 2 + [vmem] * len(qs)
    specs += ([vmem] * len(qs) if first else []) + [anywhere] * len(pieces)
    if not first:
        args += [x for s in states for x in s]
        specs += [vmem] * (3 * len(heads))
    keys = chips * 512 + (256 if first else 0)
    return pl.pallas_call(
        functools.partial(attend_kernel, heads, first, last, layout, where),
        out_shape=tuple(out_shape),
        in_specs=specs,
        out_specs=(vmem,) * len(out_shape),
        scratch_shapes=scratch,
        compiler_params=pltpu.CompilerParams(vmem_limit_bytes=40 * MIB),
        cost_estimate=pl.CostEstimate(
            flops=(8 if last else 1) * 2048 * keys * 128 * len(heads),
            bytes_accessed=4 * MIB if last else MIB,
            transcendentals=2048 * keys * len(heads) if last else 0,
        ),
        name="attend",
    )(*args)


def gather_kernel(*refs):
    pieces, out = refs[:8], refs[8]
    t = lax.axis_index("tensor")
    for n, piece in enumerate(pieces):
        h, d = n // 4, n % 4
        to = pl.multiple_of(lax.rem(t - d + 4, 4) * 2048 + h * 1024, 1024)
        out[:, pl.ds(to, 1024)] = piece[...]


def assemble(pieces):
    vmem = pl.BlockSpec(memory_space=pltpu.VMEM)
    return pl.pallas_call(
        gather_kernel,
        out_shape=jax.ShapeDtypeStruct((64, 8192), jnp.bfloat16),
        in_specs=[vmem] * 8,
        out_specs=vmem,
        compiler_params=pltpu.CompilerParams(vmem_limit_bytes=16 * MIB),
        name="assemble",
    )(*pieces)


def place(z, y, c):
    return z * 8 + y * 2 + c


def move(x, dz, dy, dc=0):
    pairs = [
        (place(z, y, c), place(z ^ dz, (y + dy) % 4, c ^ dc))
        for z in range(2)
        for y in range(4)
        for c in range(2)
    ]
    return lax.ppermute(x, "resp", pairs)


def shift(x, d):
    return lax.ppermute(x, "tensor", [(i, (i + d) % 4) for i in range(4)])


def per_device(pk, pv, queries, rk, rv, q_gain, k_gain, prompt_len, resp_len):
    plen = prompt_len[0]
    *mine, kv = split(pk, pv, queries, rk, rv)
    q_pieces = [mine[0]] + [shift(mine[d], d) for d in (1, 2, 3)]
    pair = jnp.concatenate([kv, move(kv, 1, 0)], axis=0)
    near, away = move(pair, 0, 1), move(pair, 0, 3)
    q_pieces[1], pair = lax.optimization_barrier((q_pieces[1], pair))
    pair_other = move(pair, 0, 0, 1)
    q_pieces, pair = lax.optimization_barrier((q_pieces, pair))
    opposite = move(pair, 0, 2)

    half = HEAD // 2
    pos = (plen + jnp.arange(LENGTH, dtype=jnp.int32)).astype(jnp.float32)
    freqs = jnp.power(
        jnp.float32(1000000.0), -jnp.arange(half).astype(jnp.float32) * (2.0 / HEAD)
    )
    angles = pos[:, None] * freqs[None, :]
    cosine, sine = jnp.cos(angles), jnp.sin(angles)
    c2 = jnp.concatenate([cosine, cosine], axis=1)
    s2 = jnp.concatenate([-sine, sine], axis=1)
    scale = HEAD ** (-0.5)
    tables = (
        c2 * (q_gain * scale),
        s2 * (jnp.roll(q_gain, half) * scale),
        c2 * k_gain,
        s2 * jnp.roll(k_gain, half),
    )
    q0, q1, rkv0, rkv1 = prep(q_pieces, tables)

    def send(o):
        return [o[0]] + [shift(o[d], d) for d in (1, 2, 3)]

    def both(pieces):
        return list(pieces) + [move(x, 0, 0, 1) for x in pieces]

    lens = (prompt_len, resp_len)
    layout = tuple((o, z, o, z * 256) for o in range(2) for z in range(2))
    st = attend(
        (0, 1),
        True,
        False,
        layout,
        ((0, 0), (1, 0)),
        lens,
        (q0, q1),
        (rkv0, rkv1),
        [pair, pair_other],
        None,
    )
    (near, away), st = lax.optimization_barrier(((near, away), st))
    sides = both([near, away])
    where = ((0, 3), (1, 3), (0, 1), (1, 1))
    sides_layout = tuple(
        (o * 2 + n, n * 2 + z, o, z * 256) for o in range(2) for n in range(2) for z in range(2)
    )
    st0, st1 = st[:3], st[3:]
    st0 = attend((0,), False, False, sides_layout, where, lens, (q0,), None, sides, [st0])
    st1 = attend((1,), False, False, sides_layout, where, lens, (q1,), None, sides, [st1])
    opposite, st0, st1 = lax.optimization_barrier((opposite, st0, st1))
    last = both([opposite])
    where = ((0, 2), (1, 2))
    pieces = []
    for h, q, states in ((0, q0, st0), (1, q1, st1)):
        pieces += send(
            attend((h,), False, True, layout, where, lens, (q,), None, last, [states])
        )
    return assemble(pieces)


def solution(mesh):
    rows = P(("group", "resp", "tensor"), None)
    cache = P(("group", "resp"), "tensor")
    in_specs = (cache, cache, rows, rows, rows, P(), P(), P("group"), P(("group", "resp")))
    return jax.shard_map(
        per_device, mesh=mesh, in_specs=in_specs, out_specs=rows, check_vma=False
    )
```

```python
import functools

import jax
import jax.numpy as jnp
from jax import lax
from jax.experimental import pallas as pl
from jax.experimental.pallas import tpu as pltpu
from jax.sharding import PartitionSpec as P

HEAD = 128
LENGTH = 256
ROWS = 1024
CHUNK = 1024
LOG2E = 1.4426950408889634
NEG = -1e30
MIB = 1024 * 1024


def nt(a, b):
    return lax.dot_general(a, b, (((1,), (1,)), ((), ())), preferred_element_type=jnp.float32)


def mm(a, b):
    return jnp.dot(a, b, preferred_element_type=jnp.float32)


def split_kernel(pk, pv, queries, rk, rv, own, q1, q2, q3, kv):
    t = lax.axis_index("tensor")
    for h in range(2):
        kv[:, h * 256 : h * 256 + 128] = pk[:, h * 128 : (h + 1) * 128]
        kv[:, h * 256 + 128 : h * 256 + 256] = pv[:, h * 128 : (h + 1) * 128]
    for d, dst in enumerate((own, q1, q2, q3)):
        u = lax.rem(t + d, 4)
        narrow = pl.ds(pl.multiple_of(u * 256, 256), 256)
        dst[:, :2048] = queries[:, pl.ds(pl.multiple_of(u * 2048, 2048), 2048)]
        dst[:, 2048:2304] = rk[:, narrow]
        dst[:, 2304:] = rv[:, narrow]


def split(*args):
    vmem = pl.BlockSpec(memory_space=pltpu.VMEM)
    piece = jax.ShapeDtypeStruct((64, 2560), jnp.bfloat16)
    cache = jax.ShapeDtypeStruct((256, 512), jnp.bfloat16)
    return pl.pallas_call(
        split_kernel,
        out_shape=(piece,) * 4 + (cache,),
        in_specs=[vmem] * 5,
        out_specs=(vmem,) * 5,
        compiler_params=pltpu.CompilerParams(vmem_limit_bytes=54 * MIB),
        name="split",
    )(*args)


def prep_kernel(own, r1, r2, r3, aq, bq, ak, bk, q0, q1, rkv0, rkv1):
    t = lax.axis_index("tensor")
    wide = jnp.ones((256, 128), jnp.bfloat16)
    at = lax.broadcasted_iota(jnp.int32, (128, 128), 0)
    to = lax.broadcasted_iota(jnp.int32, (128, 128), 1)
    swap = jnp.where((at - to == 64) | (to - at == 64), 1.0, 0.0).astype(jnp.bfloat16)

    def rotated(x, a, b):
        f = x.astype(jnp.float32)
        sq = f * f
        hi = sq.astype(jnp.bfloat16)
        lo = (sq - hi.astype(jnp.float32)).astype(jnp.bfloat16)
        total = mm(jnp.concatenate([hi, lo], axis=1), wide)
        r = lax.rsqrt(total * (1.0 / HEAD) + 1e-06)
        return ((f * a + mm(x, swap) * b) * r).astype(jnp.bfloat16)

    for d, piece in enumerate((own, r1, r2, r3)):
        s = lax.rem(t - d + 4, 4)
        p0 = pl.multiple_of(s * 64, 64)
        rows = pl.ds(p0, 64)
        base = (s // 2) * ROWS + lax.rem(s, 2) * 64
        a8 = jnp.concatenate([aq[rows, :]] * 8, axis=0)
        b8 = jnp.concatenate([bq[rows, :]] * 8, axis=0)
        for h, (q, rkv) in enumerate(((q0, rkv0), (q1, rkv1))):
            x = jnp.concatenate(
                [piece[:, (h * 8 + j) * 128 : (h * 8 + j + 1) * 128] for j in range(8)], axis=0
            )
            y = rotated(x, a8, b8)
            for j in range(8):
                q[pl.ds(pl.multiple_of(base + j * 128, 64), 64), :] = y[j * 64 : (j + 1) * 64]
            k = piece[:, 2048 + h * 128 : 2176 + h * 128]
            rkv[rows, 0:128] = rotated(k, ak[rows, :], bk[rows, :])
            rkv[rows, 128:256] = piece[:, 2304 + h * 128 : 2432 + h * 128]


def prep(pieces, tables):
    vmem = pl.BlockSpec(memory_space=pltpu.VMEM)
    q = jax.ShapeDtypeStruct((2048, 128), jnp.bfloat16)
    rkv = jax.ShapeDtypeStruct((256, 256), jnp.bfloat16)
    return pl.pallas_call(
        prep_kernel,
        out_shape=(q, q, rkv, rkv),
        in_specs=[vmem] * 8,
        out_specs=(vmem,) * 4,
        compiler_params=pltpu.CompilerParams(vmem_limit_bytes=16 * MIB),
        cost_estimate=pl.CostEstimate(flops=10**9, bytes_accessed=3 * 10**6, transcendentals=10**6),
        name="prep",
    )(*pieces, *tables)


def lanes(x, f, start):
    for i in range(x.shape[1] // 128):
        start = f(start, x[:, i * 128 : (i + 1) * 128])
    return start


def attend_kernel(heads, first, last, layout, where, *refs):
    it = iter(refs)
    plen_ref, rlen_ref = next(it), next(it)
    qs = [next(it) for _ in heads]
    rkvs = [next(it) for _ in heads] if first else None
    pieces = [next(it) for _ in range(1 + max(n for n, _, _, _ in layout))]
    states = [[next(it) for _ in range(3)] for _ in heads] if not first else None
    outs = [[next(it) for _ in range(4)] if last else [next(it) for _ in range(3)] for _ in heads]
    kvs, bias, m_s, mx_s, l_s, acc_s, sa, sb, oa, ob, sems = it
    plen, rlen = plen_ref[0], rlen_ref[0]
    t, r = lax.axis_index("tensor"), lax.axis_index("resp")
    core, y, z = r & 1, (r >> 1) & 3, r >> 3
    chips = len(where)
    bases = [((z ^ dz) * 4 + ((y + dy) & 3)) * 512 for dz, dy in where]
    slots, live = [], 0
    for i in range(chips):
        is_live = (bases[i] < plen).astype(jnp.int32)
        dead = i - live
        slots.append(jnp.where(is_live == 1, live, chips - 1 - dead))
        live = live + is_live
    steps = (live * 512 + CHUNK - 1) // CHUNK
    copies = []
    for m, (n, i, other, row) in enumerate(layout):
        c = 1 - core if other else core
        to = pl.multiple_of(slots[i] * 512 + c * 256, 256)
        for k, h in enumerate(heads):
            copy = pltpu.make_async_copy(
                pieces[n].at[pl.ds(row, 256), pl.ds(h * 256, 256)],
                kvs.at[k, pl.ds(to, 256), :],
                sems.at[m * len(heads) + k],
            )
            copy.start()
            copies.append(copy)
    for i in range(chips):
        at = lax.broadcasted_iota(jnp.int32, (8, 512), 1) + bases[i]
        bias[slots[i]] = jnp.where(at < plen, 0.0, NEG)

    s_bufs, o_bufs = (sa, sb), (oa, ob)
    tiles = [(k, p) for k in range(len(heads)) for p in range(2)]

    def rows_of(p):
        return slice(p * ROWS, (p + 1) * ROWS)

    def begin1(n):
        k, p = tiles[n]
        if first:
            s = nt(qs[k][rows_of(p), :], rkvs[k][:, :128])
            key = lax.broadcasted_iota(jnp.int32, (ROWS, 256), 1)
            pos = p * 128 + (lax.broadcasted_iota(jnp.int32, (ROWS, 256), 0) & 127)
            s = jnp.where((key <= pos) & (key < rlen), s, NEG)
            o_bufs[n % 2][...] = s
            m_s[...] = jnp.maximum(s[:, :128], s[:, 128:])
        else:
            m_s[...] = states[k][0][rows_of(p), :]

    def pass1(n, c):
        k, p = tiles[n]
        keys = kvs[k, pl.ds(pl.multiple_of(c * CHUNK, CHUNK), CHUNK), 0:128]
        add = jnp.concatenate([bias[2 * c], bias[2 * c + 1]], axis=1)[0:1, :]
        s = nt(qs[k][rows_of(p), :], keys) + add
        s_bufs[n % 2][c] = s
        m_s[...] = lanes(s, jnp.maximum, m_s[...])

    def weigh(s, m):
        return jnp.concatenate(
            [
                jnp.exp2((s[:, i * 128 : (i + 1) * 128] - m) * LOG2E)
                for i in range(s.shape[1] // 128)
            ],
            axis=1,
        )

    def begin2(n):
        k, p = tiles[n]
        m = jnp.broadcast_to(jnp.max(m_s[...], axis=-1, keepdims=True), (ROWS, 128))
        mx_s[...] = m
        if first:
            w = weigh(o_bufs[n % 2][...], m)
            l_s[...] = w[:, :128] + w[:, 128:]
            acc_s[...] = mm(w.astype(jnp.bfloat16), rkvs[k][:, 128:])
        else:
            old = jnp.exp2((states[k][0][rows_of(p), :] - m) * LOG2E)
            l_s[...] = states[k][1][rows_of(p), :] * old
            acc_s[...] = states[k][2][rows_of(p), :] * old

    def pass2(n, c):
        k, _ = tiles[n]
        values = kvs[k, pl.ds(pl.multiple_of(c * CHUNK, CHUNK), CHUNK), 128:256]
        w = weigh(s_bufs[n % 2][c], mx_s[...])
        l_s[...] = lanes(w, jnp.add, l_s[...])
        acc_s[...] += mm(w.astype(jnp.bfloat16), values)

    def finish(n):
        k, p = tiles[n]
        if not last:
            for ref, x in zip(outs[k], (mx_s, l_s, acc_s)):
                ref[rows_of(p), :] = x[...]
            return
        total = jnp.sum(l_s[...], axis=-1, keepdims=True)
        res = acc_s[...] / total
        pos = p * 128 + (lax.broadcasted_iota(jnp.int32, (ROWS, 128), 0) & 127)
        res = jnp.where(pos < rlen, res, 0.0).astype(jnp.bfloat16)
        for half in range(2):
            d = lax.rem(p * 2 + half - t + 4, 4)
            for e in range(4):

                @pl.when(d == e)
                def _():
                    for j in range(8):
                        r = j * 128 + half * 64
                        outs[k][e][:, j * 128 : (j + 1) * 128] = res[r : r + 64]

    begin1(0)
    for copy in copies:
        copy.wait()

    def loop(f):
        lax.fori_loop(0, steps, lambda c, z: (f(c), z)[1], 0)

    loop(lambda c: pass1(0, c))
    for n in range(len(tiles)):
        begin2(n)
        if n + 1 < len(tiles):
            begin1(n + 1)

            def both(c):
                pass1(n + 1, c)
                pass2(n, c)

            loop(both)
        else:
            loop(lambda c: pass2(n, c))
        finish(n)


def attend(heads, first, last, layout, where, lens, qs, rkvs, pieces, states):
    vmem = pl.BlockSpec(memory_space=pltpu.VMEM)
    anywhere = pl.BlockSpec(memory_space=pl.ANY)
    chips = len(where)
    state = jax.ShapeDtypeStruct((2048, 128), jnp.float32)
    if last:
        out_shape = [jax.ShapeDtypeStruct((64, 1024), jnp.bfloat16)] * (4 * len(heads))
    else:
        out_shape = [state] * (3 * len(heads))
    steps = chips * 512 // CHUNK
    f32 = jnp.float32
    scratch = [
        pltpu.VMEM((len(heads), chips * 512, 256), jnp.bfloat16),
        pltpu.VMEM((chips, 8, 512), f32),
        *[pltpu.VMEM((ROWS, 128), f32)] * 4,
        *[pltpu.VMEM((steps, ROWS, CHUNK), f32)] * 2,
        *[pltpu.VMEM((ROWS if first else 8, 256), f32)] * 2,
        pltpu.SemaphoreType.DMA((len(layout) * len(heads),)),
    ]
    args = [*lens, *qs] + (list(rkvs) if first else []) + list(pieces)
    specs = [pl.BlockSpec(memory_space=pltpu.SMEM)] * 2 + [vmem] * len(qs)
    specs += ([vmem] * len(qs) if first else []) + [anywhere] * len(pieces)
    if not first:
        args += [x for s in states for x in s]
        specs += [vmem] * (3 * len(heads))
    keys = chips * 512 + (256 if first else 0)
    return pl.pallas_call(
        functools.partial(attend_kernel, heads, first, last, layout, where),
        out_shape=tuple(out_shape),
        in_specs=specs,
        out_specs=(vmem,) * len(out_shape),
        scratch_shapes=scratch,
        compiler_params=pltpu.CompilerParams(vmem_limit_bytes=40 * MIB),
        cost_estimate=pl.CostEstimate(
            flops=(8 if last else 1) * 2048 * keys * 128 * len(heads),
            bytes_accessed=4 * MIB if last else MIB,
            transcendentals=2048 * keys * len(heads) if last else 0,
        ),
        name="attend",
    )(*args)


def gather_kernel(*refs):
    pieces, out = refs[:8], refs[8]
    t = lax.axis_index("tensor")
    for n, piece in enumerate(pieces):
        h, d = n // 4, n % 4
        to = pl.multiple_of(lax.rem(t - d + 4, 4) * 2048 + h * 1024, 1024)
        out[:, pl.ds(to, 1024)] = piece[...]


def assemble(pieces):
    vmem = pl.BlockSpec(memory_space=pltpu.VMEM)
    return pl.pallas_call(
        gather_kernel,
        out_shape=jax.ShapeDtypeStruct((64, 8192), jnp.bfloat16),
        in_specs=[vmem] * 8,
        out_specs=vmem,
        compiler_params=pltpu.CompilerParams(vmem_limit_bytes=16 * MIB),
        name="assemble",
    )(*pieces)


def place(z, y, c):
    return z * 8 + y * 2 + c


def move(x, dz, dy, dc=0):
    pairs = [
        (place(z, y, c), place(z ^ dz, (y + dy) % 4, c ^ dc))
        for z in range(2)
        for y in range(4)
        for c in range(2)
    ]
    return lax.ppermute(x, "resp", pairs)


def shift(x, d):
    return lax.ppermute(x, "tensor", [(i, (i + d) % 4) for i in range(4)])


def per_device(pk, pv, queries, rk, rv, q_gain, k_gain, prompt_len, resp_len):
    plen = prompt_len[0]
    *mine, kv = split(pk, pv, queries, rk, rv)
    q_pieces = [mine[0]] + [shift(mine[d], d) for d in (1, 2, 3)]
    pair = jnp.concatenate([kv, move(kv, 1, 0)], axis=0)
    near, away = move(pair, 0, 1), move(pair, 0, 3)
    q_pieces[1], pair = lax.optimization_barrier((q_pieces[1], pair))
    pair_other = move(pair, 0, 0, 1)

    half = HEAD // 2
    pos = (plen + jnp.arange(LENGTH, dtype=jnp.int32)).astype(jnp.float32)
    freqs = jnp.power(
        jnp.float32(1000000.0), -jnp.arange(half).astype(jnp.float32) * (2.0 / HEAD)
    )
    angles = pos[:, None] * freqs[None, :]
    cosine, sine = jnp.cos(angles), jnp.sin(angles)
    c2 = jnp.concatenate([cosine, cosine], axis=1)
    s2 = jnp.concatenate([-sine, sine], axis=1)
    scale = HEAD ** (-0.5)
    tables = (
        c2 * (q_gain * scale),
        s2 * (jnp.roll(q_gain, half) * scale),
        c2 * k_gain,
        s2 * jnp.roll(k_gain, half),
    )
    q0, q1, rkv0, rkv1 = prep(q_pieces, tables)

    def send(o):
        return [o[0]] + [shift(o[d], d) for d in (1, 2, 3)]

    def both(pieces):
        return list(pieces) + [move(x, 0, 0, 1) for x in pieces]

    lens = (prompt_len, resp_len)
    layout = tuple((o, z, o, z * 256) for o in range(2) for z in range(2))
    own, here = ((0, 0), (1, 0)), [pair, pair_other]
    st0 = attend((0,), True, False, layout, own, lens, (q0,), (rkv0,), here, None)
    (near, away, pair), st0 = lax.optimization_barrier(((near, away, pair), st0))
    opposite = move(pair, 0, 2)
    st1 = attend((1,), True, False, layout, own, lens, (q1,), (rkv1,), here, None)
    sides = both([near, away])
    where = ((0, 3), (1, 3), (0, 1), (1, 1))
    sides_layout = tuple(
        (o * 2 + n, n * 2 + z, o, z * 256) for o in range(2) for n in range(2) for z in range(2)
    )
    st0 = attend((0,), False, False, sides_layout, where, lens, (q0,), None, sides, [st0])
    st1 = attend((1,), False, False, sides_layout, where, lens, (q1,), None, sides, [st1])
    opposite, st0, st1 = lax.optimization_barrier((opposite, st0, st1))
    last = both([opposite])
    where = ((0, 2), (1, 2))
    pieces = []
    for h, q, states in ((0, q0, st0), (1, q1, st1)):
        pieces += send(
            attend((h,), False, True, layout, where, lens, (q,), None, last, [states])
        )
    return assemble(pieces)


def solution(mesh):
    rows = P(("group", "resp", "tensor"), None)
    cache = P(("group", "resp"), "tensor")
    in_specs = (cache, cache, rows, rows, rows, P(), P(), P("group"), P(("group", "resp")))
    return jax.shard_map(
        per_device, mesh=mesh, in_specs=in_specs, out_specs=rows, check_vma=False
    )
```

```python
import functools

import jax
import jax.numpy as jnp
from jax import lax
from jax.experimental import pallas as pl
from jax.experimental.pallas import tpu as pltpu
from jax.sharding import PartitionSpec as P

HEAD = 128
LENGTH = 256
ROWS = 1024
CHUNK = 1024
LOG2E = 1.4426950408889634
NEG = -1e30
MIB = 1024 * 1024


def nt(a, b):
    return lax.dot_general(a, b, (((1,), (1,)), ((), ())), preferred_element_type=jnp.float32)


def mm(a, b):
    return jnp.dot(a, b, preferred_element_type=jnp.float32)


def split_kernel(pk, pv, queries, rk, rv, own, q1, q2, q3, kv):
    t = lax.axis_index("tensor")
    for h in range(2):
        kv[:, h * 256 : h * 256 + 128] = pk[:, h * 128 : (h + 1) * 128]
        kv[:, h * 256 + 128 : h * 256 + 256] = pv[:, h * 128 : (h + 1) * 128]
    for d, dst in enumerate((own, q1, q2, q3)):
        u = lax.rem(t + d, 4)
        narrow = pl.ds(pl.multiple_of(u * 256, 256), 256)
        dst[:, :2048] = queries[:, pl.ds(pl.multiple_of(u * 2048, 2048), 2048)]
        dst[:, 2048:2304] = rk[:, narrow]
        dst[:, 2304:] = rv[:, narrow]


def split(*args):
    vmem = pl.BlockSpec(memory_space=pltpu.VMEM)
    piece = jax.ShapeDtypeStruct((64, 2560), jnp.bfloat16)
    cache = jax.ShapeDtypeStruct((256, 512), jnp.bfloat16)
    return pl.pallas_call(
        split_kernel,
        out_shape=(piece,) * 4 + (cache,),
        in_specs=[vmem] * 5,
        out_specs=(vmem,) * 5,
        compiler_params=pltpu.CompilerParams(vmem_limit_bytes=54 * MIB),
        name="split",
    )(*args)


def prep_kernel(own, r1, r2, r3, aq, bq, ak, bk, q0, q1, rkv0, rkv1):
    t = lax.axis_index("tensor")
    wide = jnp.ones((256, 128), jnp.bfloat16)
    at = lax.broadcasted_iota(jnp.int32, (128, 128), 0)
    to = lax.broadcasted_iota(jnp.int32, (128, 128), 1)
    swap = jnp.where((at - to == 64) | (to - at == 64), 1.0, 0.0).astype(jnp.bfloat16)

    def rotated(x, a, b):
        f = x.astype(jnp.float32)
        sq = f * f
        hi = sq.astype(jnp.bfloat16)
        lo = (sq - hi.astype(jnp.float32)).astype(jnp.bfloat16)
        total = mm(jnp.concatenate([hi, lo], axis=1), wide)
        r = lax.rsqrt(total * (1.0 / HEAD) + 1e-06)
        return ((f * a + mm(x, swap) * b) * r).astype(jnp.bfloat16)

    for d, piece in enumerate((own, r1, r2, r3)):
        s = lax.rem(t - d + 4, 4)
        p0 = pl.multiple_of(s * 64, 64)
        rows = pl.ds(p0, 64)
        base = (s // 2) * ROWS + lax.rem(s, 2) * 64
        a8 = jnp.concatenate([aq[rows, :]] * 8, axis=0)
        b8 = jnp.concatenate([bq[rows, :]] * 8, axis=0)
        for h, (q, rkv) in enumerate(((q0, rkv0), (q1, rkv1))):
            x = jnp.concatenate(
                [piece[:, (h * 8 + j) * 128 : (h * 8 + j + 1) * 128] for j in range(8)], axis=0
            )
            y = rotated(x, a8, b8)
            for j in range(8):
                q[pl.ds(pl.multiple_of(base + j * 128, 64), 64), :] = y[j * 64 : (j + 1) * 64]
            k = piece[:, 2048 + h * 128 : 2176 + h * 128]
            rkv[rows, 0:128] = rotated(k, ak[rows, :], bk[rows, :])
            rkv[rows, 128:256] = piece[:, 2304 + h * 128 : 2432 + h * 128]


def prep(pieces, tables):
    vmem = pl.BlockSpec(memory_space=pltpu.VMEM)
    q = jax.ShapeDtypeStruct((2048, 128), jnp.bfloat16)
    rkv = jax.ShapeDtypeStruct((256, 256), jnp.bfloat16)
    return pl.pallas_call(
        prep_kernel,
        out_shape=(q, q, rkv, rkv),
        in_specs=[vmem] * 8,
        out_specs=(vmem,) * 4,
        compiler_params=pltpu.CompilerParams(vmem_limit_bytes=16 * MIB),
        cost_estimate=pl.CostEstimate(flops=10**9, bytes_accessed=3 * 10**6, transcendentals=10**6),
        name="prep",
    )(*pieces, *tables)


def lanes(x, f, start):
    for i in range(x.shape[1] // 128):
        start = f(start, x[:, i * 128 : (i + 1) * 128])
    return start


def attend_kernel(heads, first, last, layout, where, *refs):
    it = iter(refs)
    plen_ref, rlen_ref = next(it), next(it)
    qs = [next(it) for _ in heads]
    rkvs = [next(it) for _ in heads] if first else None
    pieces = [next(it) for _ in range(1 + max(n for n, _, _, _ in layout))]
    states = [[next(it) for _ in range(3)] for _ in heads] if not first else None
    outs = [[next(it) for _ in range(4)] if last else [next(it) for _ in range(3)] for _ in heads]
    kvs, bias, m_s, mx_s, l_s, acc_s, sa, sb, oa, ob, sems = it
    plen, rlen = plen_ref[0], rlen_ref[0]
    t, r = lax.axis_index("tensor"), lax.axis_index("resp")
    core, y, z = r & 1, (r >> 1) & 3, r >> 3
    chips = len(where)
    bases = [((z ^ dz) * 4 + ((y + dy) & 3)) * 512 for dz, dy in where]
    slots, live = [], 0
    for i in range(chips):
        is_live = (bases[i] < plen).astype(jnp.int32)
        dead = i - live
        slots.append(jnp.where(is_live == 1, live, chips - 1 - dead))
        live = live + is_live
    steps = (live * 512 + CHUNK - 1) // CHUNK
    copies = []
    for m, (n, i, other, row) in enumerate(layout):
        c = 1 - core if other else core
        to = pl.multiple_of(slots[i] * 512 + c * 256, 256)
        for k, h in enumerate(heads):
            copy = pltpu.make_async_copy(
                pieces[n].at[pl.ds(row, 256), pl.ds(h * 256, 256)],
                kvs.at[k, pl.ds(to, 256), :],
                sems.at[m * len(heads) + k],
            )
            copy.start()
            copies.append(copy)
    for i in range(chips):
        at = lax.broadcasted_iota(jnp.int32, (8, 512), 1) + bases[i]
        bias[slots[i]] = jnp.where(at < plen, 0.0, NEG)

    s_bufs, o_bufs = (sa, sb), (oa, ob)
    tiles = [(k, p) for k in range(len(heads)) for p in range(2)]

    def rows_of(p):
        return slice(p * ROWS, (p + 1) * ROWS)

    def begin1(n):
        k, p = tiles[n]
        if first:
            s = nt(qs[k][rows_of(p), :], rkvs[k][:, :128])
            key = lax.broadcasted_iota(jnp.int32, (ROWS, 256), 1)
            pos = p * 128 + (lax.broadcasted_iota(jnp.int32, (ROWS, 256), 0) & 127)
            s = jnp.where((key <= pos) & (key < rlen), s, NEG)
            o_bufs[n % 2][...] = s
            m_s[...] = jnp.maximum(s[:, :128], s[:, 128:])
        else:
            m_s[...] = states[k][0][rows_of(p), :]

    def pass1(n, c, start=0, count=ROWS):
        k, p = tiles[n]
        part = pl.ds(start, count)
        keys = kvs[k, pl.ds(pl.multiple_of(c * CHUNK, CHUNK), CHUNK), 0:128]
        add = jnp.concatenate([bias[2 * c], bias[2 * c + 1]], axis=1)[0:1, :]
        s = nt(qs[k][pl.ds(p * ROWS + start, count), :], keys) + add
        s_bufs[n % 2][c, part, :] = s
        m_s[part, :] = lanes(s, jnp.maximum, m_s[part, :])

    def weigh(s, m):
        return jnp.concatenate(
            [
                jnp.exp2((s[:, i * 128 : (i + 1) * 128] - m) * LOG2E)
                for i in range(s.shape[1] // 128)
            ],
            axis=1,
        )

    def begin2(n):
        k, p = tiles[n]
        m = jnp.broadcast_to(jnp.max(m_s[...], axis=-1, keepdims=True), (ROWS, 128))
        mx_s[...] = m
        if first:
            w = weigh(o_bufs[n % 2][...], m)
            l_s[...] = w[:, :128] + w[:, 128:]
            acc_s[...] = mm(w.astype(jnp.bfloat16), rkvs[k][:, 128:])
        else:
            old = jnp.exp2((states[k][0][rows_of(p), :] - m) * LOG2E)
            l_s[...] = states[k][1][rows_of(p), :] * old
            acc_s[...] = states[k][2][rows_of(p), :] * old

    def pass2(n, c, start=0, count=ROWS):
        k, _ = tiles[n]
        part = pl.ds(start, count)
        values = kvs[k, pl.ds(pl.multiple_of(c * CHUNK, CHUNK), CHUNK), 128:256]
        w = weigh(s_bufs[n % 2][c, part, :], mx_s[part, :])
        l_s[part, :] = lanes(w, jnp.add, l_s[part, :])
        acc_s[part, :] += mm(w.astype(jnp.bfloat16), values)

    def finish(n):
        k, p = tiles[n]
        if not last:
            for ref, x in zip(outs[k], (mx_s, l_s, acc_s)):
                ref[rows_of(p), :] = x[...]
            return
        total = jnp.sum(l_s[...], axis=-1, keepdims=True)
        res = acc_s[...] / total
        pos = p * 128 + (lax.broadcasted_iota(jnp.int32, (ROWS, 128), 0) & 127)
        res = jnp.where(pos < rlen, res, 0.0).astype(jnp.bfloat16)
        for half in range(2):
            d = lax.rem(p * 2 + half - t + 4, 4)
            for e in range(4):

                @pl.when(d == e)
                def _():
                    for j in range(8):
                        r = j * 128 + half * 64
                        outs[k][e][:, j * 128 : (j + 1) * 128] = res[r : r + 64]

    begin1(0)
    for copy in copies:
        copy.wait()

    def loop(f):
        lax.fori_loop(0, steps, lambda c, z: (f(c), z)[1], 0)

    def halves(f):
        half = ROWS // 2

        def step(i, x):
            f(i >> 1, pl.multiple_of((i & 1) * half, half), half)
            return x

        lax.fori_loop(0, 2 * steps, step, 0)

    halves(lambda c, start, count: pass1(0, c, start, count))
    for n in range(len(tiles)):
        begin2(n)
        if n + 1 < len(tiles):
            begin1(n + 1)

            def both(c):
                pass1(n + 1, c)
                pass2(n, c)

            loop(both)
        else:
            halves(lambda c, start, count: pass2(n, c, start, count))
        finish(n)


def attend(heads, first, last, layout, where, lens, qs, rkvs, pieces, states):
    vmem = pl.BlockSpec(memory_space=pltpu.VMEM)
    anywhere = pl.BlockSpec(memory_space=pl.ANY)
    chips = len(where)
    state = jax.ShapeDtypeStruct((2048, 128), jnp.float32)
    if last:
        out_shape = [jax.ShapeDtypeStruct((64, 1024), jnp.bfloat16)] * (4 * len(heads))
    else:
        out_shape = [state] * (3 * len(heads))
    steps = chips * 512 // CHUNK
    f32 = jnp.float32
    scratch = [
        pltpu.VMEM((len(heads), chips * 512, 256), jnp.bfloat16),
        pltpu.VMEM((chips, 8, 512), f32),
        *[pltpu.VMEM((ROWS, 128), f32)] * 4,
        *[pltpu.VMEM((steps, ROWS, CHUNK), f32)] * 2,
        *[pltpu.VMEM((ROWS if first else 8, 256), f32)] * 2,
        pltpu.SemaphoreType.DMA((len(layout) * len(heads),)),
    ]
    args = [*lens, *qs] + (list(rkvs) if first else []) + list(pieces)
    specs = [pl.BlockSpec(memory_space=pltpu.SMEM)] * 2 + [vmem] * len(qs)
    specs += ([vmem] * len(qs) if first else []) + [anywhere] * len(pieces)
    if not first:
        args += [x for s in states for x in s]
        specs += [vmem] * (3 * len(heads))
    keys = chips * 512 + (256 if first else 0)
    return pl.pallas_call(
        functools.partial(attend_kernel, heads, first, last, layout, where),
        out_shape=tuple(out_shape),
        in_specs=specs,
        out_specs=(vmem,) * len(out_shape),
        scratch_shapes=scratch,
        compiler_params=pltpu.CompilerParams(vmem_limit_bytes=40 * MIB),
        cost_estimate=pl.CostEstimate(
            flops=(8 if last else 1) * 2048 * keys * 128 * len(heads),
            bytes_accessed=4 * MIB if last else MIB,
            transcendentals=2048 * keys * len(heads) if last else 0,
        ),
        name="attend",
    )(*args)


def gather_kernel(*refs):
    pieces, out = refs[:8], refs[8]
    t = lax.axis_index("tensor")
    for n, piece in enumerate(pieces):
        h, d = n // 4, n % 4
        to = pl.multiple_of(lax.rem(t - d + 4, 4) * 2048 + h * 1024, 1024)
        out[:, pl.ds(to, 1024)] = piece[...]


def assemble(pieces):
    vmem = pl.BlockSpec(memory_space=pltpu.VMEM)
    return pl.pallas_call(
        gather_kernel,
        out_shape=jax.ShapeDtypeStruct((64, 8192), jnp.bfloat16),
        in_specs=[vmem] * 8,
        out_specs=vmem,
        compiler_params=pltpu.CompilerParams(vmem_limit_bytes=16 * MIB),
        name="assemble",
    )(*pieces)


def place(z, y, c):
    return z * 8 + y * 2 + c


def move(x, dz, dy, dc=0):
    pairs = [
        (place(z, y, c), place(z ^ dz, (y + dy) % 4, c ^ dc))
        for z in range(2)
        for y in range(4)
        for c in range(2)
    ]
    return lax.ppermute(x, "resp", pairs)


def shift(x, d):
    return lax.ppermute(x, "tensor", [(i, (i + d) % 4) for i in range(4)])


def per_device(pk, pv, queries, rk, rv, q_gain, k_gain, prompt_len, resp_len):
    plen = prompt_len[0]
    *mine, kv = split(pk, pv, queries, rk, rv)
    q_pieces = [mine[0]] + [shift(mine[d], d) for d in (1, 2, 3)]
    pair = jnp.concatenate([kv, move(kv, 1, 0)], axis=0)
    near, away = move(pair, 0, 1), move(pair, 0, 3)
    q_pieces[1], pair = lax.optimization_barrier((q_pieces[1], pair))
    pair_other = move(pair, 0, 0, 1)

    half = HEAD // 2
    pos = (plen + jnp.arange(LENGTH, dtype=jnp.int32)).astype(jnp.float32)
    freqs = jnp.power(
        jnp.float32(1000000.0), -jnp.arange(half).astype(jnp.float32) * (2.0 / HEAD)
    )
    angles = pos[:, None] * freqs[None, :]
    cosine, sine = jnp.cos(angles), jnp.sin(angles)
    c2 = jnp.concatenate([cosine, cosine], axis=1)
    s2 = jnp.concatenate([-sine, sine], axis=1)
    scale = HEAD ** (-0.5)
    tables = (
        c2 * (q_gain * scale),
        s2 * (jnp.roll(q_gain, half) * scale),
        c2 * k_gain,
        s2 * jnp.roll(k_gain, half),
    )
    q0, q1, rkv0, rkv1 = prep(q_pieces, tables)

    def send(o):
        return [o[0]] + [shift(o[d], d) for d in (1, 2, 3)]

    def both(pieces):
        return list(pieces) + [move(x, 0, 0, 1) for x in pieces]

    lens = (prompt_len, resp_len)
    layout = tuple((o, z, o, z * 256) for o in range(2) for z in range(2))
    own, here = ((0, 0), (1, 0)), [pair, pair_other]
    st0 = attend((0,), True, False, layout, own, lens, (q0,), (rkv0,), here, None)
    (near, away, pair), st0 = lax.optimization_barrier(((near, away, pair), st0))
    opposite = move(pair, 0, 2)
    st1 = attend((1,), True, False, layout, own, lens, (q1,), (rkv1,), here, None)
    sides = both([near, away])
    where = ((0, 3), (1, 3), (0, 1), (1, 1))
    sides_layout = tuple(
        (o * 2 + n, n * 2 + z, o, z * 256) for o in range(2) for n in range(2) for z in range(2)
    )
    st0 = attend((0,), False, False, sides_layout, where, lens, (q0,), None, sides, [st0])
    st1 = attend((1,), False, False, sides_layout, where, lens, (q1,), None, sides, [st1])
    opposite, st0, st1 = lax.optimization_barrier((opposite, st0, st1))
    last = both([opposite])
    where = ((0, 2), (1, 2))
    pieces = []
    for h, q, states in ((0, q0, st0), (1, q1, st1)):
        pieces += send(
            attend((h,), False, True, layout, where, lens, (q,), None, last, [states])
        )
    return assemble(pieces)


def solution(mesh):
    rows = P(("group", "resp", "tensor"), None)
    cache = P(("group", "resp"), "tensor")
    in_specs = (cache, cache, rows, rows, rows, P(), P(), P("group"), P(("group", "resp")))
    return jax.shard_map(
        per_device, mesh=mesh, in_specs=in_specs, out_specs=rows, check_vma=False
    )
```
